32 devices in a mesh: dp: 16 (over z, y, x), branch: 2 (over core).
Axes of the slice: x: 2, y: 2, z: 4, core: 2. Of those that a mesh axis runs over, the one named last changes fastest.
Arguments:
- features: bfloat16 [24576, 602], P('dp'), may hold values from -6 to 6
- labels: int32 [121, 24576], P(None, 'dp'), may hold values 0 or 1
- label_mask: int32 [24576], P('dp'), may hold values 0 or 1
- graph_sizes: int32 [16], P('dp'), may hold values from 512 to 1536, as said below
- block_index: int32 [192, 8], P('dp'), may hold values from 0 to 11
- block_mask: int32 [192, 8], P('dp'), may hold values 0 or 1
- edge_weight: bfloat16 [192, 8, 128, 128], P('dp'), may hold values from 0 to 0.001953125
- step_count: int32 [1], replicated, may hold values from 2 to 20
- branch_weight: float32 [3, 2, 512, 512], P(None, 'branch'), may hold values from -0.25 to 0.25
- branch_moment: float32 [3, 2, 512, 512], P(None, 'branch'), may hold values from -0.00024414062 to 0.00024414062
- concat_weight: float32 [3, 1024, 512], P(None, 'branch'), may hold values from -0.1875 to 0.1875
- concat_moment: float32 [3, 1024, 512], P(None, 'branch'), may hold values from -0.00024414062 to 0.00024414062
- input_weight: float32 [602, 512], replicated, may hold values from -0.25 to 0.25
- input_moment: float32 [602, 512], replicated, may hold values from -2.670288e-05 to 2.670288e-05
- input_second: float32 [602, 512], replicated, may hold values from 2.692882e-13 to 1.0508807e-12
- head_weight: float32 [121, 512], replicated, may hold values from -6 to 6
- head_moment: float32 [121, 512], replicated, may hold values from -3.33786e-06 to 3.33786e-06
- head_second: float32 [121, 512], replicated, may hold values from 4.1253583e-15 to 1.628431e-14
Outputs:
- loss: float32 [], replicated
- branch_new: float32 [3, 2, 512, 512], P(None, 'branch')
- branch_next: float32 [3, 2, 512, 512], P(None, 'branch')
- concat_new: float32 [3, 1024, 512], P(None, 'branch')
- concat_next: float32 [3, 1024, 512], P(None, 'branch')
- input_new: float32 [602, 512], replicated
- input_first: float32 [602, 512], replicated
- input_next: float32 [602, 512], replicated
- head_new: float32 [121, 512], replicated
- head_first: float32 [121, 512], replicated
- head_next: float32 [121, 512], replicated
The draws below stay inside these ranges and needn't reach their ends.
Inputs may be any that keep to these rules, and one draw needn't show every extreme that they name: `graph_sizes`: some subgraph has exactly 1536 nodes.
All inputs are finite; a program needn't handle non-finite values. No bound on the sum of `labels` or of `label_mask` or of `block_mask` on one device may be relied on, other than what follows from the above.
Results may differ from the reference program's by a relative error of at most 0.015.
Values may be sent and summed in bfloat16 or wider, within the bound.
No kernel may reach another device: no remote copies, remote signals or barrier semaphores. Data moves between devices by JAX's collectives and lax.ppermute only.
A program may use at most 256 MiB of HBM per device.

```python
import math
import jax
import jax.numpy as jnp
from jax import lax

D = 512
F_IN = 602
LAB = 121
LAYERS = 3
NS_STEPS = 5
BLK = 128
KB = 8
NMAX = 1536
NB = 12
GRAPHS = 16


def draw_graph_sizes(key, part):
    drawn = jax.random.randint(key, (GRAPHS,), NMAX // 3, NMAX + 1)
    largest = jax.random.randint(jax.random.fold_in(key, 7), (), 0, GRAPHS)
    return jnp.where(jnp.arange(GRAPHS) == largest, NMAX, drawn).astype(jnp.int32)


def touch_ends(entries, own_key, low, high):
    longest = entries.shape.index(max(entries.shape))
    spots = []
    for shift in (0, 1):
        where = [jax.random.randint(jax.random.fold_in(own_key, axis), (), 0, length) for axis, length in enumerate(entries.shape)]
        where[longest] = (where[longest] + shift) % entries.shape[longest]
        spots.append(tuple(where))
    return entries.at[spots[0]].set(low).at[spots[1]].set(high)


def block_levels(key, shape, split, low, top_value):
    loudness = 1.0
    for axis_at, blocks in split:
        heights = jax.random.uniform(jax.random.fold_in(jax.random.fold_in(key, 6), axis_at), (blocks,), jnp.float32, low / len(split), top_value / len(split))
        loudness = loudness * jnp.repeat(jnp.exp(heights), shape[axis_at] // blocks).reshape((-1,) + (1,) * (len(shape) - 1 - axis_at))
    return loudness


def scatter_about(key, shape, deviation, most, pieces=(), kind=jnp.bfloat16):
    values = deviation * jax.random.normal(key, shape, jnp.float32)
    if pieces:
        values = values * block_levels(key, shape, pieces, -0.22, 0.18)
    return jnp.clip(values, -most, most).astype(kind)


def setup_inputs(seed: int = 0) -> dict:
    streams_of = jax.random.split(jax.random.key(seed), 19)
    return {
        "features": scatter_about(streams_of[0], (GRAPHS * NMAX, F_IN), 1.0, 6.0, ((0, 16),)),
        "labels": touch_ends((jax.random.randint(streams_of[1], (LAB, GRAPHS * NMAX), 0, 2) < 1).astype(jnp.int32), jax.random.fold_in(streams_of[1], 1), 0, 1),
        "label_mask": touch_ends((jax.random.randint(streams_of[2], (GRAPHS * NMAX,), 0, 2) < 1).astype(jnp.int32), jax.random.fold_in(streams_of[2], 1), 0, 1),
        "graph_sizes": draw_graph_sizes(jax.random.fold_in(streams_of[18], 71), 0),
        "block_index": touch_ends(jax.random.randint(streams_of[4], (GRAPHS * NB, KB), 0, NB), jax.random.fold_in(streams_of[4], 1), 0, NB - 1).astype(jnp.int32),
        "block_mask": touch_ends((jax.random.randint(streams_of[5], (GRAPHS * NB, KB), 0, 4) < 3).astype(jnp.int32), jax.random.fold_in(streams_of[5], 1), 0, 1),
        "edge_weight": jnp.clip(0.001953125 * jax.random.uniform(streams_of[6], (GRAPHS * NB, KB, BLK, BLK), jnp.float32) ** block_levels(streams_of[6], (GRAPHS * NB, KB, BLK, BLK), ((0, 16),), -0.2, 0.2), 0.0, 0.001953125).astype(jnp.bfloat16),
        "step_count": jax.random.randint(streams_of[7], (1,), 2, 21).astype(jnp.int32),
        "branch_weight": scatter_about(streams_of[8], (LAYERS, 2, D, D), D ** -0.5, 0.25, ((1, 2),), jnp.float32),
        "branch_moment": scatter_about(streams_of[9], (LAYERS, 2, D, D), (0.7 * (LAB * D * GRAPHS * NMAX) ** -0.5), 0.00024414062, ((1, 2),), jnp.float32),
        "concat_weight": scatter_about(streams_of[10], (LAYERS, 2 * D, D), (2 * D) ** -0.5, 0.1875, ((1, 2),), jnp.float32),
        "concat_moment": scatter_about(streams_of[11], (LAYERS, 2 * D, D), (0.7 * (LAB * D * GRAPHS * NMAX) ** -0.5), 0.00024414062, ((1, 2),), jnp.float32),
        "input_weight": scatter_about(streams_of[12], (F_IN, D), F_IN ** -0.5, 0.25, (), jnp.float32),
        "input_moment": scatter_about(streams_of[13], (F_IN, D), (0.07 * (LAB * D * GRAPHS * NMAX) ** -0.5), 2.6702880859375e-05, (), jnp.float32),
        "input_second": jnp.clip(jnp.exp(jax.random.uniform(streams_of[14], (F_IN, D), jnp.float32, math.log(2.6928819959505523e-13), math.log(1.050880736597204e-12))), 2.6928819959505523e-13, 1.050880736597204e-12),
        "head_weight": scatter_about(streams_of[15], (LAB, D), 1.0, 6.0, (), jnp.float32),
        "head_moment": scatter_about(streams_of[16], (LAB, D), (0.1 * (LAB * LAB * D * GRAPHS * NMAX) ** -0.5), 3.337860107421875e-06, (), jnp.float32),
        "head_second": jnp.clip(jnp.exp(jax.random.uniform(streams_of[17], (LAB, D), jnp.float32, math.log(4.1253583496047696e-15), math.log(1.6284310054917595e-14))), 4.1253583496047696e-15, 1.6284310054917595e-14),
    }


@jax.custom_vjp
def low(v):
    return lax.optimization_barrier(v.astype(jnp.bfloat16)).astype(jnp.float32)

@jax.custom_vjp
def low_back(v):
    return v

def low_keep(v):
    return (low(v), None)

def low_pass(kept, grad):
    return (grad,)

def back_keep(v):
    return (v, None)

def back_low(kept, grad):
    return (low(grad),)
low.defvjp(low_keep, low_pass)
low_back.defvjp(back_keep, back_low)
highest = lax.Precision.HIGHEST
quintic_one = 3.4445
quintic_two = -4.775
quintic_three = 2.0315
norm_epsilon = 1e-06
momentum_decay = 0.95
muon_rate = 0.5
first_decay = 0.9
second_decay = 0.999
adam_epsilon = 1e-08
weight_decay = 0.01

def product(left, right):
    return jnp.dot(left, right, precision=highest, preferred_element_type=jnp.float32)

def graph_loss(params, graph, loss_scale):
    input_weight, branch_weight, concat_weight, head_weight = params
    features, labels, label_mask, graph_size, block_index, block_mask, edge_weight = graph
    inside = (jnp.arange(NMAX) < graph_size).astype(jnp.float32)[:, None]
    counted = label_mask.astype(jnp.float32) * inside[:, 0]
    weighted = edge_weight * block_mask.astype(jnp.float32)[:, :, None, None]
    hidden = low_back(product(features, low(input_weight))) * inside
    for layer_index in range(LAYERS):
        rounded = low(hidden)
        blocks = rounded.reshape(NB, BLK, D)[block_index]
        gathered = jnp.einsum('ikrc,ikcd->ird', weighted, blocks, precision=highest).reshape(NMAX, D)
        neighbour = low(low_back(gathered))
        self_out = low(low_back(product(rounded, low(branch_weight[layer_index, 0]))))
        neigh_out = low(low_back(product(neighbour, low(branch_weight[layer_index, 1]))))
        joined = product(jnp.concatenate([self_out, neigh_out], 1), low(concat_weight[layer_index]))
        activated = jax.nn.silu(low_back(joined))
        hidden = activated * lax.rsqrt(lax.optimization_barrier(jnp.sum(activated * activated, 1, keepdims=True)) + norm_epsilon) * inside
    logits = low_back(product(low(head_weight), low(hidden).T))
    losses = jax.nn.softplus(logits) - labels.astype(jnp.float32) * logits
    return jnp.sum(losses * counted[None, :]) * loss_scale

def orthogonalize(moment):
    scaled = moment / (jnp.sqrt(lax.optimization_barrier(jnp.sum(moment * moment, axis=(1, 2), keepdims=True))) + 1e-07)
    for sweep in range(NS_STEPS):
        gram = jnp.einsum('mij,mik->mjk', scaled, scaled, precision=highest)
        poly = quintic_two * gram + quintic_three * jnp.einsum('mij,mjk->mik', gram, gram, precision=highest)
        scaled = quintic_one * scaled + jnp.einsum('mij,mjk->mik', scaled, poly, precision=highest)
    return scaled

def adamw(weight, moment, second, grad, rate, steps):
    moment = first_decay * moment + (1.0 - first_decay) * grad
    second = second_decay * second + (1.0 - second_decay) * grad * grad
    corrected = moment / (1.0 - jnp.power(first_decay, steps)) / (jnp.sqrt(second / (1.0 - jnp.power(second_decay, steps))) + adam_epsilon)
    return (weight - rate * (corrected + weight_decay * weight), moment, second)

def reference(features, labels, label_mask, graph_sizes, block_index, block_mask, edge_weight, step_count, branch_weight, branch_moment, concat_weight, concat_moment, input_weight, input_moment, input_second, head_weight, head_moment, head_second):
    graphs = (features.astype(jnp.float32).reshape(GRAPHS, NMAX, F_IN), labels.reshape(LAB, GRAPHS, NMAX).transpose(1, 0, 2), label_mask.reshape(GRAPHS, NMAX), graph_sizes, block_index.reshape(GRAPHS, NB, KB), block_mask.reshape(GRAPHS, NB, KB), edge_weight.astype(jnp.float32).reshape(GRAPHS, NB, KB, BLK, BLK))
    inside_all = (jnp.arange(NMAX)[None, :] < graph_sizes[:, None]).astype(jnp.float32)
    count = jnp.sum(label_mask.reshape(GRAPHS, NMAX).astype(jnp.float32) * inside_all)
    loss_scale = 1.0 / (jnp.maximum(count, 1.0) * LAB)
    params = (input_weight, branch_weight, concat_weight, head_weight)

    def total_loss(params):

        def one_graph(carry, graph):
            return (carry + graph_loss(params, graph, loss_scale), None)
        total, unused = lax.scan(jax.checkpoint(one_graph), jnp.zeros((), jnp.float32), graphs)
        return total
    loss, pullback = jax.vjp(total_loss, params)
    grad_input, grad_branch, grad_concat, grad_head = pullback(jnp.ones((), jnp.float32))[0]
    branch_next = momentum_decay * branch_moment + grad_branch
    branch_ortho = orthogonalize(branch_next.reshape(LAYERS * 2, D, D)).reshape(branch_next.shape)
    branch_new = branch_weight - muon_rate * (branch_ortho + weight_decay * branch_weight)
    concat_next = momentum_decay * concat_moment + grad_concat
    concat_ortho = orthogonalize(concat_next)
    concat_new = concat_weight - muon_rate * (jnp.sqrt(2.0) * concat_ortho + weight_decay * concat_weight)
    steps = step_count[0].astype(jnp.float32)
    input_new, input_first, input_next = adamw(input_weight, input_moment, input_second, grad_input, 0.02, steps)
    head_new, head_first, head_next = adamw(head_weight, head_moment, head_second, grad_head, 0.5, steps)
    return (loss, branch_new, branch_next, concat_new, concat_next, input_new, input_first, input_next, head_new, head_first, head_next)
```

```python
import functools
import jax
import jax.numpy as jnp
from jax import lax
from jax.experimental import pallas as pl
from jax.experimental.pallas import tpu as pltpu
from jax.sharding import PartitionSpec as P

NS_STEPS = 5
WIDTH = 512
HALF = WIDTH // 2
BLK = 128
LABPAD = 128
SUB = 256

quintic_one = 3.4445
quintic_two = -4.775
quintic_three = 2.0315
norm_epsilon = 1e-06
momentum_decay = 0.95
muon_rate = 0.5
first_decay = 0.9
second_decay = 0.999
adam_epsilon = 1e-08
weight_decay = 0.01

F32 = jnp.float32
BF16 = jnp.bfloat16
MB = 1 << 20
VM = pltpu.VMEM
DMA = pltpu.SemaphoreType.DMA
WIDE = 2 * WIDTH


def nn(a, b):
    return jnp.dot(a, b, preferred_element_type=F32)


def nt(a, b):
    return lax.dot_general(a, b, (((1,), (1,)), ((), ())), preferred_element_type=F32)


def tn(a, b):
    return lax.dot_general(a, b, (((0,), (0,)), ((), ())), preferred_element_type=F32)


def vmem():
    return pl.BlockSpec(memory_space=VM)


def smem():
    return pl.BlockSpec(memory_space=pltpu.SMEM)


def anywhere():
    return pl.BlockSpec(memory_space=pl.ANY)


def in_hbm():
    return pl.BlockSpec(memory_space=pltpu.HBM)


def far(x):
    return pltpu.with_memory_space_constraint(x, pltpu.HBM)


def shaped(*shape, dtype=BF16):
    return jax.ShapeDtypeStruct(shape, dtype)


def params(limit):
    return pltpu.CompilerParams(vmem_limit_bytes=limit * MB)


def cost(us):
    return pl.CostEstimate(flops=int(us), bytes_accessed=1, transcendentals=0)


def moved(src, dst, sem):
    cp = pltpu.make_async_copy(src, dst, sem)
    cp.start()
    return cp


def picked(first, a, b, dst, sem):
    @pl.when(first)
    def _():
        pltpu.make_async_copy(a, dst, sem).start()

    @pl.when(jnp.logical_not(first))
    def _():
        pltpu.make_async_copy(b, dst, sem).start()

    return pltpu.make_async_copy(a, dst, sem)


def cast_kernel(branch_ref, concat_ref, out_ref):
    out_ref[0, 0] = branch_ref[0, 0].astype(BF16)
    out_ref[1, 0] = concat_ref[0].astype(BF16)


def cast_weights(branch_weight, concat_weight):
    layers = branch_weight.shape[0]
    return pl.pallas_call(
        cast_kernel,
        grid=(layers,),
        in_specs=[
            pl.BlockSpec((1, 1, WIDTH, WIDTH), lambda l: (l, 0, 0, 0)),
            pl.BlockSpec((1, WIDTH, WIDTH), lambda l: (l, 0, 0)),
        ],
        out_specs=pl.BlockSpec((2, 1, WIDTH, WIDTH), lambda l: (0, l, 0, 0)),
        out_shape=pltpu.HBM((2, layers, WIDTH, WIDTH), BF16),
        compiler_params=params(16),
        cost_estimate=cost(4),
        name="weights",
    )(far(branch_weight), far(concat_weight))


def build_kernel(index_ref, mask_ref, size_ref, edge_ref, feat_ref, win_ref, adj_ref, hid_ref, acc_ref, win):
    step = pl.program_id(0)
    per, kb = edge_ref.shape[0], edge_ref.shape[1]

    @pl.when(step == 0)
    def _():
        win[...] = win_ref[...].astype(BF16)

    for i in range(per):
        acc_ref[...] = jnp.zeros_like(acc_ref)
        for k in range(kb):
            at = pl.multiple_of(index_ref[step * per + i, k] * BLK, BLK)
            keep = mask_ref[step * per + i, k].astype(F32)
            acc_ref[:, pl.ds(at, BLK)] += edge_ref[i, k].astype(F32) * keep
        adj_ref[i * BLK : (i + 1) * BLK, :] = acc_ref[...].astype(BF16)
    size = per * BLK
    inside = lax.broadcasted_iota(jnp.int32, (size, 1), 0) + step * size < size_ref[0]
    hidden = tn(feat_ref[...], win[...])
    hid_ref[...] = jnp.where(inside, hidden, 0.0).astype(BF16)


def build(block_index, block_mask, graph_sizes, edge_weight, features_t, input_weight):
    nb, kb = block_index.shape
    feats, rows = features_t.shape
    per = 2
    return pl.pallas_call(
        build_kernel,
        grid=(nb // per,),
        in_specs=[
            smem(),
            smem(),
            smem(),
            pl.BlockSpec((per, kb, BLK, BLK), lambda i: (i, 0, 0, 0)),
            pl.BlockSpec((feats, per * BLK), lambda i: (0, i)),
            pl.BlockSpec((feats, WIDTH), lambda i: (0, 0)),
        ],
        out_specs=[
            pl.BlockSpec((per * BLK, rows), lambda i: (i, 0)),
            pl.BlockSpec((per * BLK, WIDTH), lambda i: (i, 0)),
        ],
        out_shape=[pltpu.HBM((rows, rows), BF16), pltpu.HBM((rows, WIDTH), BF16)],
        scratch_shapes=[VM((BLK, rows), F32), VM((feats, WIDTH), BF16)],
        compiler_params=params(32),
        cost_estimate=cost(8),
        name="adjacency",
    )(block_index, block_mask, graph_sizes, far(edge_weight), far(features_t), far(input_weight))


def inside_of(size_ref, at, tile):
    return lax.broadcasted_iota(jnp.int32, (tile, 1), 0) + at < size_ref[0]


def joined_back(joined, grad, inside):
    grad = jnp.where(inside, grad, 0.0)
    sigma = jax.nn.sigmoid(joined)
    activated = joined * sigma
    inverse = lax.rsqrt(jnp.sum(activated * activated, 1, keepdims=True) + norm_epsilon)
    along = jnp.sum(activated * grad, 1, keepdims=True)
    grad_act = inverse * grad - (inverse * inverse * inverse * along) * activated
    return (grad_act * sigma * (1.0 + joined * (1.0 - sigma))).astype(BF16)


def weight_grads(core, low, incat, outcat, gj, gcat, send_ref, keep_ref):
    mine = pl.ds(pl.multiple_of(core * WIDTH, WIDTH), WIDTH)
    branch = tn(incat[:, mine], gcat[:, mine])
    concat = tn(outcat[:, mine], gj[...])
    send_ref[...] = jnp.where(low, concat, branch).astype(BF16)
    keep_ref[...] = jnp.where(low, branch, concat)


def layer_tile_back(joined, grad, inside, c_ref, w1_ref, rows, gj, gcat, gagg):
    g = joined_back(joined, grad, inside)
    gj[rows, :] = g
    both = nt(g, c_ref[...]).astype(BF16)
    gcat[rows, :] = both
    gagg[rows, :] = nt(both[:, WIDTH:], w1_ref[...]).astype(BF16)


def forward_kernel(
    layers,
    tile,
    core_ref,
    side_ref,
    size_ref,
    adj_hbm,
    hid_hbm,
    own_hbm,
    other_hbm,
    head_ref,
    labels_ref,
    mask_ref,
    *refs,
):
    kept = layers - 1
    in_out = refs[:kept]
    out_out = refs[kept : 2 * kept]
    join_out = refs[2 * kept : 3 * kept]
    send_hbm, keep_hbm, ghead_hbm, totals_hbm, gself_hbm, gagg_hbm = refs[3 * kept : 3 * kept + 6]
    refs = refs[3 * kept + 6 :]
    incat = [refs[l % 2] for l in range(layers)]
    outcat = [refs[2 + l % 2] for l in range(layers)]
    adj, w, c, joined, last, head, gl, glb, gj, send, keep, ghead_ref, totals_ref, sems, out_sems, end_sems = refs[4:]
    gcat, gagg = adj.at[:, pl.ds(0, WIDE)], adj.at[:, pl.ds(WIDE, WIDTH)]
    core = core_ref[0]
    other = 1 - core
    rows_total = adj.shape[0]
    tiles = rows_total // tile
    own_rows = pl.ds(pl.multiple_of(core * WIDTH, WIDTH), WIDTH)
    other_rows = pl.ds(pl.multiple_of(other * WIDTH, WIDTH), WIDTH)

    hid_cp = moved(hid_hbm, incat[0].at[:, pl.ds(0, WIDTH)], sems.at[0])
    adj_cps = [
        moved(adj_hbm.at[pl.ds(t * tile, tile)], adj.at[pl.ds(t * tile, tile)], sems.at[1 + t]) for t in range(tiles)
    ]
    weight_cps = []
    for l in range(layers):
        base = 1 + tiles + 4 * l
        weight_cps.append(
            [
                moved(own_hbm.at[0, l], w.at[l, core], sems.at[base]),
                moved(other_hbm.at[0, l], w.at[l, other], sems.at[base + 1]),
                moved(own_hbm.at[1, l], c.at[l, own_rows, :], sems.at[base + 2]),
                moved(other_hbm.at[1, l], c.at[l, other_rows, :], sems.at[base + 3]),
            ]
        )
    labs, width = head_ref.shape
    head[...] = jnp.zeros_like(head)
    head[0:labs, :] = head_ref[...].astype(BF16)
    lane = lax.broadcasted_iota(jnp.int32, (1, rows_total), 1)
    counted_all = jnp.where(lane < size_ref[0], mask_ref[...].astype(F32), 0.0)
    hid_cp.wait()
    stores = []
    for l in range(layers):
        src, dst, jo = incat[l], outcat[l], joined.at[l % 2]
        if l >= 2:
            stores[l - 2][1].wait()
            stores[l - 2][2].wait()
        for t in range(tiles):
            rows = pl.ds(t * tile, tile)
            if l == 0:
                adj_cps[t].wait()
            neigh = nn(adj[rows, :], src[:, 0:WIDTH]).astype(BF16)
            src[rows, WIDTH:] = neigh
            if t == 0:
                for cp in weight_cps[l]:
                    cp.wait()
            dst[rows, 0:WIDTH] = nn(src[rows, 0:WIDTH], w[l, 0]).astype(BF16)
            dst[rows, WIDTH:] = nn(neigh, w[l, 1]).astype(BF16)
            for u in range(0, tile, SUB):
                part = pl.ds(t * tile + u, SUB)
                j = nn(dst[part, :], c[l])
                jo[part, :] = j
                activated = j * jax.nn.sigmoid(j)
                inverse = lax.rsqrt(jnp.sum(activated * activated, 1, keepdims=True) + norm_epsilon)
                inverse = jnp.where(inside_of(size_ref, t * tile + u, SUB), inverse, 0.0)
                hidden = (activated * inverse).astype(BF16)
                if 1 <= l < layers - 1 and t == 0 and u == 0:
                    stores[l - 1][0].wait()
                if l + 1 < layers:
                    incat[l + 1][part, 0:WIDTH] = hidden
                else:
                    last[part, :] = hidden
        if l < kept:
            pairs = ((src, in_out[l]), (dst, out_out[l]), (jo, join_out[l]))
            stores.append([moved(a, b, out_sems.at[3 * l + n]) for n, (a, b) in enumerate(pairs)])

    gl[...] = jnp.zeros_like(gl)
    loss = jnp.zeros((1, 1), F32)
    for t in range(tiles):
        rows = pl.ds(t * tile, tile)
        lanes = slice(t * tile, (t + 1) * tile)
        logits = nt(head[...], last[rows, :])[:labs]
        targets = labels_ref[:, lanes].astype(F32)
        counted = counted_all[:, lanes]
        small = jnp.exp(-jnp.abs(logits))
        ratio = 1.0 / (1.0 + small)
        sigma = jnp.where(logits >= 0.0, ratio, small * ratio)
        soft = jnp.maximum(logits, 0.0) + jnp.log1p(small)
        per_node = jnp.sum(soft - targets * logits, 0, keepdims=True)
        loss = loss + jnp.sum(per_node * counted, 1, keepdims=True)
        gl[0:labs, lanes] = counted * (sigma - targets)
    glb[...] = gl[...].astype(BF16)
    totals_ref[0:4, :] = jnp.broadcast_to(loss, (4, 128))
    totals_ref[4:8, :] = jnp.broadcast_to(jnp.sum(counted_all, 1, keepdims=True), (4, 128))
    ghead = nn(glb[...], last[:, pl.ds(pl.multiple_of(core * HALF, HALF), HALF)])
    mid = LABPAD // 2
    ghead_ref[:, 0:HALF] = ghead[:mid]
    ghead_ref[:, HALF:] = ghead[mid:]

    l = layers - 1
    jo = joined.at[l % 2]
    for t in range(tiles):
        rows = pl.ds(t * tile, tile)
        grad = tn(glb[:, t * tile : (t + 1) * tile], head[...])
        inside = inside_of(size_ref, t * tile, tile)
        layer_tile_back(jo[rows, :], grad, inside, c.at[l], w.at[l, 1], rows, gj, gcat, gagg)
    outs = [
        moved(gcat.at[:, pl.ds(0, WIDTH)], gself_hbm, end_sems.at[0]),
        moved(gagg, gagg_hbm, end_sems.at[1]),
        moved(ghead_ref, ghead_hbm, end_sems.at[4]),
        moved(totals_ref, totals_hbm, end_sems.at[5]),
    ]
    weight_grads(core, side_ref[0] == 0, incat[l], outcat[l], gj, gcat, send, keep)
    outs += [moved(send, send_hbm, end_sems.at[2]), moved(keep, keep_hbm, end_sems.at[3])]
    for cp in outs:
        cp.wait()
    for n, group in enumerate(stores):
        for cp in group if n + 2 >= layers else []:
            cp.wait()


def forward(core, side, size, adj, hid, own, other, head, labels, mask, layers):
    rows = adj.shape[0]
    kept = layers - 1
    tile = rows // 2
    wide = pltpu.HBM((rows, WIDE), BF16)
    out_shape = (
        [wide] * (2 * kept)
        + [pltpu.HBM((rows, WIDTH), F32)] * kept
        + [
            pltpu.HBM((WIDTH, WIDTH), BF16),
            pltpu.HBM((WIDTH, WIDTH), F32),
            pltpu.HBM((LABPAD // 2, WIDTH), F32),
            pltpu.HBM((8, BLK), F32),
            pltpu.HBM((rows, WIDTH), BF16),
            pltpu.HBM((rows, WIDTH), BF16),
        ]
    )
    return pl.pallas_call(
        functools.partial(forward_kernel, layers, tile),
        in_specs=[smem()] * 3 + [in_hbm()] * 4 + [vmem()] * 3,
        out_specs=[in_hbm()] * (3 * kept + 6),
        out_shape=out_shape,
        scratch_shapes=[VM((rows, WIDE), BF16)] * 4
        + [
            VM((rows, rows), BF16),
            VM((layers, 2, WIDTH, WIDTH), BF16),
            VM((layers, WIDE, WIDTH), BF16),
            VM((2, rows, WIDTH), F32),
            VM((rows, WIDTH), BF16),
            VM((LABPAD, WIDTH), BF16),
            VM((LABPAD, rows), F32),
            VM((LABPAD, rows), BF16),
            VM((rows, WIDTH), BF16),
            VM((WIDTH, WIDTH), BF16),
            VM((WIDTH, WIDTH), F32),
            VM((LABPAD // 2, WIDTH), F32),
            VM((8, BLK), F32),
            DMA((1 + rows // tile + 4 * layers,)),
            DMA((3 * kept,)),
            DMA((6,)),
        ],
        compiler_params=params(42),
        cost_estimate=cost(30),
        name="forward",
    )(core, side, size, far(adj), far(hid), far(own), far(other), head, labels, mask)


def backward_kernel(layers, l, tile, core_ref, side_ref, size_ref, *refs):
    adj_hbm, own_hbm, other_hbm, joined_hbm, incat_hbm, outcat_hbm, gself_hbm, gagg_hbm = refs[:8]
    refs = refs[8:]
    if l:
        send_hbm, keep_hbm, totals_hbm, send_ref, keep_ref, gself_out, gagg_out, token_ref = refs[:8]
        refs = refs[8:]
    else:
        feat_hbm, ghead_hbm, send_ref, keep_ref, token_ref = refs[:5]
        w0, feat, first_grad, rest, last_sems = refs[-5:]
        refs = refs[5:-5]
    adj, wself, w1, c, joined, incat, outcat, gj, gcat, gself_in, gagg_in, gagg, totals, sems, adj_sems, join_sems = refs
    token_ref[...] = jnp.zeros_like(token_ref)
    core = core_ref[0]
    other = 1 - core
    low = side_ref[0] == 0
    tiles = adj.shape[0] // tile
    first = core == 0

    def load_tile(t):
        rows = pl.ds(t * tile, tile)
        return (
            moved(adj_hbm.at[:, rows], adj.at[:, rows], adj_sems.at[t]),
            moved(joined_hbm.at[rows], joined.at[rows], join_sems.at[t]),
        )

    early = [
        moved(gagg_hbm, gagg_in, sems.at[6]),
        picked(first, own_hbm.at[0, l + 1], other_hbm.at[0, l + 1], wself, sems.at[0]),
        moved(gself_hbm, gself_in, sems.at[7]),
    ]
    tile_cps = [load_tile(0)]
    own_rows = pl.ds(pl.multiple_of(core * WIDTH, WIDTH), WIDTH)
    other_rows = pl.ds(pl.multiple_of(other * WIDTH, WIDTH), WIDTH)
    weight_cps = [
        picked(first, other_hbm.at[0, l], own_hbm.at[0, l], w1, sems.at[1]),
        moved(own_hbm.at[1, l], c.at[own_rows, :], sems.at[2]),
        moved(other_hbm.at[1, l], c.at[other_rows, :], sems.at[3]),
    ]
    if l == 1:
        early.append(moved(totals_hbm, totals, sems.at[12]))
    for cp in early:
        cp.wait()
    if l == 1:
        put_totals(send_ref, keep_ref.shape[0], totals[...])
    done = keep_hbm.shape[0] if l else 0
    late, outs = [], []
    for t in range(tiles):
        rows = pl.ds(t * tile, tile)
        tile_cps[t][0].wait()
        if t + 1 < tiles:
            tile_cps.append(load_tile(t + 1))
        if t == 0:
            late += [moved(incat_hbm, incat, sems.at[4]), moved(outcat_hbm, outcat, sems.at[5])]
            if l:
                late += [
                    moved(send_hbm.at[pl.ds(0, done)], send_ref.at[pl.ds(0, done)], sems.at[8]),
                    moved(keep_hbm, keep_ref.at[pl.ds(0, done)], sems.at[9]),
                ]
            else:
                late += [
                    picked(first, own_hbm.at[0, 0], other_hbm.at[0, 0], w0, last_sems.at[0]),
                    moved(feat_hbm, feat, last_sems.at[1]),
                ]
        grad = tn(adj[:, rows], gagg_in[...]) + nt(gself_in[rows, :], wself[...])
        tile_cps[t][1].wait()
        if t == 0:
            for cp in weight_cps:
                cp.wait()
        inside = inside_of(size_ref, t * tile, tile)
        layer_tile_back(joined[rows, :], grad, inside, c, w1, rows, gj, gcat, gagg)
    if l:
        outs = [
            moved(gcat.at[:, pl.ds(0, WIDTH)], gself_out, sems.at[10]),
            moved(gagg, gagg_out, sems.at[11]),
        ]
    for cp in late:
        cp.wait()
    here = slice(done, done + WIDTH)
    weight_grads(core, low, incat, outcat, gj, gcat, send_ref.at[here], keep_ref.at[here])
    for cp in outs:
        cp.wait()
    if l:
        return
    feats = feat.shape[0]
    mid = LABPAD // 2
    tall = pl.cdiv(feats, BLK) * BLK // 2
    rest[...] = jnp.zeros_like(rest)
    head_cp = moved(ghead_hbm, rest.at[pl.ds(tall, mid)], last_sems.at[2])
    mine = pl.ds(pl.multiple_of(core * HALF, HALF), HALF)
    for t in range(tiles):
        rows = pl.ds(t * tile, tile)
        grad = tn(adj[:, rows], gagg[:, mine]) + nt(gcat[rows, 0:WIDTH], w0[mine, :])
        grad = jnp.where(inside_of(size_ref, t * tile, tile), grad, 0.0)
        first_grad[rows, :] = grad.astype(BF16)
    grad = nn(feat[...], first_grad[...])
    rest[0:tall, 0:HALF] = grad[0:tall]
    rest[0 : feats - tall, HALF:] = grad[tall:]
    head_cp.wait()
    half = rest.shape[0] // 2
    upper, lower = rest[0:half, :], rest[half:, :]
    send_ref[WIDTH:, :] = jnp.where(low, lower, upper).astype(BF16)
    keep_ref[WIDTH:, :] = jnp.where(low, upper, lower)


def backward(core, side, size, shared, kept, extra, layers, l):
    rows = shared[0].shape[0]
    tile = rows // 2
    scratch = [
        VM((rows, rows), BF16),
        VM((WIDTH, WIDTH), BF16),
        VM((WIDTH, WIDTH), BF16),
        VM((WIDE, WIDTH), BF16),
        VM((rows, WIDTH), F32),
        VM((rows, WIDE), BF16),
        VM((rows, WIDE), BF16),
        VM((rows, WIDTH), BF16),
        VM((rows, WIDE), BF16),
        VM((rows, WIDTH), BF16),
        VM((rows, WIDTH), BF16),
        VM((rows, WIDTH), BF16),
        VM((8, BLK), F32),
        DMA((13,)),
        DMA((rows // tile,)),
        DMA((rows // tile,)),
    ]
    token = shaped(8, BLK, dtype=F32)
    if l:
        tall = WIDTH * (layers - l)
        more = EXTRA if l == 1 else 0
        hbm = pltpu.HBM((rows, WIDTH), BF16)
        out_shape = [shaped(tall + more, WIDTH), shaped(tall, WIDTH, dtype=F32), hbm, hbm, token]
        out_specs = [vmem()] * 2 + [in_hbm()] * 2 + [vmem()]
    else:
        feats = extra[0].shape[0]
        tall = pl.cdiv(feats, BLK) * BLK // 2
        unit = 8 * lax.axis_size("dp")
        out = pl.cdiv(WIDTH + (tall + LABPAD // 2 + 1) // 2, unit) * unit
        rest = 2 * (out - WIDTH)
        out_shape = [shaped(out, WIDTH), shaped(out, WIDTH, dtype=F32), token]
        out_specs = [vmem()] * 3
        scratch += [
            VM((WIDTH, WIDTH), BF16),
            VM((feats, rows), BF16),
            VM((rows, HALF), BF16),
            VM((rest, WIDTH), F32),
            DMA((3,)),
        ]
    args = [far(x) for x in (*shared, *kept, *extra)]
    return pl.pallas_call(
        functools.partial(backward_kernel, layers, l, tile),
        in_specs=[smem()] * 3 + [in_hbm()] * len(args),
        out_specs=out_specs,
        out_shape=out_shape,
        scratch_shapes=scratch,
        compiler_params=params(36),
        cost_estimate=cost(15),
        name=f"backward{l}",
    )(core, side, size, *args)


def muon_kernel(
    layers,
    l,
    core_ref,
    side_ref,
    scale_ref,
    mine_hbm,
    got_hbm,
    swap_hbm,
    mb_hbm,
    mc_hbm,
    other_mb_hbm,
    other_mc_hbm,
    wb_hbm,
    wc_hbm,
    token_in,
    *refs,
):
    above = l < layers - 1
    if above:
        ortho_ref = refs[4]
        refs = refs[5:]
    bnext_hbm, cnext_hbm, bnew_hbm, cnew_hbm, sent_out, token_ref = refs[:6]
    gb, gc, gs, mb, mc, ms, wk, wa, x, sems = refs[6:]
    token_ref[...] = jnp.zeros_like(token_ref)
    first = core_ref[0] == 0
    low_side = side_ref[0] == 0
    scale = scale_ref[0]
    cps = [
        picked(low_side, mine_hbm, got_hbm, gb, sems.at[0]),
        picked(low_side, got_hbm, mine_hbm, gc, sems.at[1]),
        moved(mb_hbm.at[l, 0], mb, sems.at[2]),
        moved(mc_hbm.at[l], mc, sems.at[3]),
        moved(swap_hbm, gs, sems.at[4]),
        picked(first, other_mc_hbm.at[l], other_mb_hbm.at[l, 0], ms, sems.at[5]),
    ]
    late = picked(first, wc_hbm.at[l], wb_hbm.at[l, 0], wk, sems.at[6])
    if above:
        above_cp = picked(first, wb_hbm.at[l + 1, 0], wc_hbm.at[l + 1], wa, sems.at[10])
    for cp in cps:
        cp.wait()
    mb[...] = momentum_decay * mb[...] + scale * gb[...].astype(F32)
    mc[...] = momentum_decay * mc[...] + scale * gc[...].astype(F32)
    stores = [moved(mb, bnext_hbm.at[l, 0], sems.at[7]), moved(mc, cnext_hbm.at[l], sems.at[8])]
    ms[...] = momentum_decay * ms[...] + scale * gs[...].astype(F32)
    if above:
        above_cp.wait()
        other_gain = jnp.where(first, 1.0, 2.0**0.5)
        wa[...] = wa[...] - muon_rate * (other_gain * ortho_ref[...].astype(F32) + weight_decay * wa[...])
        stores.append(picked_out(first, wa, bnew_hbm.at[l + 1, 0], cnew_hbm.at[l + 1], sems.at[11]))

    a = jnp.where(first, mc[...], mb[...])
    b = ms[...]
    na, nb = jnp.sum(a * a), jnp.sum(b * b)
    link = jnp.where(first, 1.0, 0.0)
    x[0:WIDTH, :] = a * (1.0 / (jnp.sqrt(jnp.full((1, 1), na + link * nb, F32)) + 1e-07))
    x[WIDTH:, :] = b * (1.0 / (jnp.sqrt(jnp.full((1, 1), nb + link * na, F32)) + 1e-07))

    def sweep(blocks, shift):
        zero = quintic_one + quintic_two * shift + quintic_three * shift * shift
        slope = quintic_two + 2.0 * quintic_three * shift
        low = [x[block, :].astype(BF16) for block in blocks]
        grams = []
        for v in low:
            left, right = v[:, :HALF], v[:, HALF:]
            grams.append((tn(left, left), tn(left, right), tn(right, right)))
        if shift:
            at = lax.broadcasted_iota(jnp.int32, (HALF, HALF), 0) == lax.broadcasted_iota(jnp.int32, (HALF, HALF), 1)
            eye = jnp.where(at, shift, 0.0)
            grams = [(g - eye, h, k - eye) for g, h, k in grams]
        polys = []
        for gram in grams:
            corner, side, tail = [g.astype(BF16) for g in gram]
            top = jnp.concatenate([corner, side], 1)
            bottom = jnp.concatenate([side.T, tail], 1)
            squares = (nt(top, top), nt(top, bottom), nt(bottom, bottom))
            corner, side, tail = [(slope * g + quintic_three * q).astype(BF16) for g, q in zip(gram, squares)]
            top = jnp.concatenate([corner, side], 1)
            polys.append(jnp.concatenate([top, jnp.concatenate([side.T, tail], 1)], 0))
        for block, v, p in zip(blocks, low, polys):
            x[block, :] = zero * x[block, :] + nn(v, p)

    def sweeps(blocks):
        @pl.loop(0, NS_STEPS - 1)
        def _(step):
            sweep(blocks, 0.0)

        sweep(blocks, 0.75)

    @pl.when(first)
    def _():
        sweeps([slice(0, WIDE)])

    @pl.when(jnp.logical_not(first))
    def _():
        sweeps([slice(0, WIDTH), slice(WIDTH, WIDE)])

    sent_out[...] = x[WIDTH:, :].astype(BF16)
    late.wait()
    gain = jnp.where(first, 2.0**0.5, 1.0)
    wk[...] = wk[...] - muon_rate * (gain * x[0:WIDTH, :] + weight_decay * wk[...])
    stores.append(picked_out(first, wk, cnew_hbm.at[l], bnew_hbm.at[l, 0], sems.at[9]))
    for cp in stores:
        cp.wait()


def picked_out(first, src, a, b, sem):
    @pl.when(first)
    def _():
        pltpu.make_async_copy(src, a, sem).start()

    @pl.when(jnp.logical_not(first))
    def _():
        pltpu.make_async_copy(src, b, sem).start()

    return pltpu.make_async_copy(src, a, sem)


def muon(core, side, scale, mine, got, swap, moments, weights, token, kept, ortho, layers, l):
    square = VM((WIDTH, WIDTH), F32)
    low = VM((WIDTH, WIDTH), BF16)
    args = [core, side, scale, mine, got, swap, *[far(x) for x in (*moments, *weights)], token, *kept, *ortho]
    return pl.pallas_call(
        functools.partial(muon_kernel, layers, l),
        in_specs=[smem()] * 3 + [anywhere()] * 3 + [in_hbm()] * 6 + [anywhere()] + [in_hbm()] * len(kept) + [vmem()] * len(ortho),
        out_specs=[in_hbm()] * 4 + [vmem()] * 2,
        out_shape=[
            pltpu.HBM((layers, 1, WIDTH, WIDTH), F32),
            pltpu.HBM((layers, WIDTH, WIDTH), F32),
            pltpu.HBM((layers, 1, WIDTH, WIDTH), F32),
            pltpu.HBM((layers, WIDTH, WIDTH), F32),
            shaped(WIDTH, WIDTH),
            shaped(8, BLK, dtype=F32),
        ],
        input_output_aliases={13 + n: n for n in range(len(kept))},
        scratch_shapes=[low, low, low, square, square, square, square, square, VM((WIDE, WIDTH), F32), DMA((12,))],
        compiler_params=params(24),
        cost_estimate=cost(13),
        name="muon",
    )(*args)


def adam_step(weight, moment, second, grad, rate, first_fix, second_fix):
    moment = first_decay * moment + (1.0 - first_decay) * grad
    second = second_decay * second + (1.0 - second_decay) * grad * grad
    corrected = (moment * first_fix) / (jnp.sqrt(second * second_fix) + adam_epsilon)
    return (weight - rate * (corrected + weight_decay * weight), moment, second)


def adam_kernel(core_ref, numbers_ref, own_ref, other_ref, wb_hbm, wc_hbm, bnew_in, cnew_in, ortho_ref, *refs):
    bnew_hbm, cnew_hbm, grad, wk, sems = refs[12:]
    first = core_ref[0] == 0
    load = picked(first, wb_hbm.at[0, 0], wc_hbm.at[0], wk, sems.at[0])
    scale, first_fix, second_fix = numbers_ref[0], numbers_ref[1], numbers_ref[2]
    tall = grad.shape[0] // 2
    mid = LABPAD // 2
    core = core_ref[0]
    for ref, at in ((own_ref, core), (other_ref, 1 - core)):
        lanes = pl.ds(pl.multiple_of(at * HALF, HALF), HALF)
        grad[0:mid, lanes] = ref[tall : tall + mid, 0:HALF].astype(F32)
        grad[mid:LABPAD, lanes] = ref[tall : tall + mid, HALF:].astype(F32)
    labs = refs[3].shape[0]
    outs = adam_step(refs[3][...], refs[4][...], refs[5][...], scale * grad[0:labs, :], 0.5, first_fix, second_fix)
    for ref, value in zip(refs[9:12], outs):
        ref[...] = value
    load.wait()
    gain = jnp.where(first, 1.0, 2.0**0.5)
    wk[...] = wk[...] - muon_rate * (gain * ortho_ref[...].astype(F32) + weight_decay * wk[...])
    store = picked_out(first, wk, bnew_hbm.at[0, 0], cnew_hbm.at[0], sems.at[1])
    for ref, at in ((own_ref, core), (other_ref, 1 - core)):
        lanes = pl.ds(pl.multiple_of(at * HALF, HALF), HALF)
        grad[0:tall, lanes] = ref[0:tall, 0:HALF].astype(F32)
        grad[tall : 2 * tall, lanes] = ref[0:tall, HALF:].astype(F32)
    feats = refs[0].shape[0]
    outs = adam_step(refs[0][...], refs[1][...], refs[2][...], scale * grad[0:feats, :], 0.02, first_fix, second_fix)
    for ref, value in zip(refs[6:9], outs):
        ref[...] = value
    store.wait()


def adam(core, numbers, own, other, weights, bnew, cnew, ortho, inputs, heads):
    tall = pl.cdiv(inputs[0].shape[0], BLK) * BLK // 2
    shapes = [shaped(*x.shape, dtype=F32) for x in (*inputs, *heads)]
    shapes += [pltpu.HBM(x.shape, F32) for x in (bnew, cnew)]
    return pl.pallas_call(
        adam_kernel,
        in_specs=[smem(), smem()] + [vmem()] * 2 + [in_hbm()] * 4 + [vmem()] * 7,
        out_specs=[vmem()] * 6 + [in_hbm()] * 2,
        out_shape=shapes,
        input_output_aliases={6: 6, 7: 7},
        scratch_shapes=[VM((2 * tall, WIDTH), F32), VM((WIDTH, WIDTH), F32), DMA((2,))],
        compiler_params=params(24),
        cost_estimate=cost(4),
        name="adam",
    )(core, numbers, own, other, *[far(x) for x in weights], bnew, cnew, ortho, *inputs, *heads)


def across_cores(x):
    return lax.ppermute(x, "branch", [(0, 1), (1, 0)])


def rounds():
    bits = lax.axis_size("dp").bit_length() - 1
    first = [(b,) for b in range(min(bits, 2))] + [tuple(range(b, min(b + 2, bits))) for b in range(2, bits, 2)]
    second = first[:]
    if bits >= 2:
        second[0], second[1] = first[1], first[0]
    return list(zip(first, second))


def mask_of(bits, m):
    return sum(1 << b for n, b in enumerate(bits) if m >> n & 1)


def paired(x, both, m):
    pairs = [(i * 2 + c, (i ^ mask_of(both[c], m)) * 2 + c) for i in range(lax.axis_size("dp")) for c in range(2)]
    return lax.ppermute(x, ("dp", "branch"), pairs)


def sides_of(core, place):
    def index(bits):
        return sum(((place >> b) & 1) << n for n, b in enumerate(bits))

    return [jnp.where(core == 0, index(a), index(b)).astype(jnp.int32).reshape(1) for a, b in rounds()]


EXTRA = 16


def put_totals(send_ref, at, totals):
    high = totals.astype(BF16)
    left = totals - high.astype(F32)
    mid = left.astype(BF16)
    low = (left - mid.astype(F32)).astype(BF16)
    send_ref[at : at + EXTRA, 0:BLK] = jnp.concatenate([high, high], 0)
    send_ref[at : at + EXTRA, BLK : 2 * BLK] = jnp.concatenate([mid, mid], 0)
    send_ref[at : at + EXTRA, 2 * BLK : 3 * BLK] = jnp.concatenate([low, low], 0)
    send_ref[at : at + EXTRA, 3 * BLK :] = jnp.zeros((EXTRA, BLK), BF16)


def get_totals(got_ref, at):
    rows = got_ref[at : at + EXTRA, :].astype(F32)
    return (rows[0:8, 0:BLK] + rows[0:8, BLK : 2 * BLK]) + rows[0:8, 2 * BLK : 3 * BLK]


def scatter_step(ins, outs, more):
    side_ref, keep_ref = ins[:2]
    gots = ins[2 : len(ins) - more]
    n = keep_ref.shape[0]
    if more:
        totals = ins[-1][...]
        for got in gots:
            totals = totals + get_totals(got, n)
        outs[-1][...] = totals
        outs = outs[:-1]

    def summed(rows):
        value = keep_ref[rows, :]
        for got in gots:
            value = value + got[rows, :].astype(F32)
        return value

    if len(outs) == 1:
        outs[0][...] = summed(slice(0, n)).astype(BF16)
        return
    parts = len(outs)
    size = n // parts
    side = side_ref[0]

    def give(place):
        for m in range(1, parts):
            at = (place ^ m) * size
            outs[m - 1][0:size, :] = summed(slice(at, at + size)).astype(BF16)
        outs[-1][...] = summed(slice(place * size, place * size + size))

    for place in range(parts):
        pl.when(side == place)(functools.partial(give, place))
    if more:
        for m in range(1, parts):
            put_totals(outs[m - 1], size, totals)


def gather_step(ins, outs):
    side_ref, blocks = ins[0], ins[1:]
    n = blocks[0].shape[0]
    parts = len(blocks)

    def join(place):
        at = 0
        for ref in outs:
            done = 0
            while done < ref.shape[0]:
                block, inner = (at + done) // n, (at + done) % n
                size = min(n - inner, ref.shape[0] - done)
                ref[done : done + size, :] = blocks[block ^ place][inner : inner + size, :]
                done += size
            at += ref.shape[0]

    for place in range(parts):
        pl.when(side_ref[0] == place)(functools.partial(join, place))


def choose_step(ins, outs):
    flag_ref, mine_ref, got_ref = ins

    @pl.when(flag_ref[0] != 0)
    def _():
        outs[0][...] = mine_ref[...]

    @pl.when(flag_ref[0] == 0)
    def _():
        outs[0][...] = got_ref[...]


def pass_step(ins, outs):
    outs[0][...] = ins[1][...]


STEPS = {
    "scatter": lambda ins, outs: scatter_step(ins, outs, 0),
    "scatter_more": lambda ins, outs: scatter_step(ins, outs, 1),
    "gather": gather_step,
    "choose": choose_step,
    "pass": pass_step,
}


def joint_kernel(plan, token_in, *refs):
    ins_total = sum(n for _, n, _ in plan)
    ins, outs = refs[:ins_total], refs[ins_total:]
    outs[-1][...] = jnp.zeros_like(outs[-1])
    for kind, n_in, n_out in plan:
        STEPS[kind](ins[:n_in], outs[:n_out])
        ins, outs = ins[n_in:], outs[n_out:]


def joint(token, *jobs):
    plan = [(kind, 1 + len(arrays), len(shapes)) for kind, _, arrays, shapes in jobs]
    in_specs, args, out_shape = [anywhere()], [token], []
    for _, side, arrays, shapes in jobs:
        in_specs += [smem()] + [vmem()] * len(arrays)
        args += [side, *arrays]
        out_shape += shapes
    out_shape.append(shaped(8, BLK, dtype=F32))
    outs = pl.pallas_call(
        functools.partial(joint_kernel, plan),
        in_specs=in_specs,
        out_specs=[vmem()] * len(out_shape),
        out_shape=out_shape,
        compiler_params=params(8),
        cost_estimate=cost(0.5),
        name="step",
    )(*args)
    results = []
    for _, _, _, shapes in jobs:
        results.append(outs[: len(shapes)])
        outs = outs[len(shapes) :]
    return outs[0], results


class Summing:
    def __init__(self, send, keep, sides, totals, sizes):
        self.sends, self.keep, self.sides, self.totals, self.sizes = [send], keep, sides, totals, sizes
        self.rounds = rounds()
        self.at = 0

    def exchange(self, which, blocks):
        return [paired(x, self.rounds[which], m + 1) for m, x in enumerate(blocks)]

    def partners(self, which):
        return (1 << len(self.rounds[which][0])) - 1

    def job(self):
        count = len(self.rounds)
        at = self.at
        if at < count:
            gots = self.exchange(at, self.sends)
            n = self.keep.shape[0]
            arrays, shapes, side = [self.keep, *gots], [shaped(n, WIDTH)], self.sides[0]
            if at < count - 1:
                others = self.partners(at + 1)
                size = n // (others + 1)
                extra = 0 if self.totals is None else EXTRA
                shapes = [shaped(size + extra, WIDTH)] * others + [shaped(size, WIDTH, dtype=F32)]
                side = self.sides[at + 1]
            if self.totals is None:
                return "scatter", side, arrays, shapes
            return "scatter_more", side, [*arrays, self.totals], [*shapes, shaped(8, BLK, dtype=F32)]
        which = 2 * count - 1 - at
        others = self.partners(which)
        gots = self.exchange(which, [self.mine] * others)
        sizes = self.sizes if which == 1 else [(others + 1) * self.mine.shape[0]]
        return "gather", self.sides[which], [self.mine, *gots], [shaped(n, WIDTH) for n in sizes]

    def take(self, results):
        count = len(self.rounds)
        if self.at < count:
            if self.totals is not None:
                *results, self.totals = results
            if self.at < count - 1:
                *self.sends, self.keep = results
            else:
                self.mine = results[0]
        else:
            self.mine = results[0]
        if self.at == 2 * count - 2:
            self.mine = results
            self.got = [self.exchange(0, [part])[0] for part in results]
        self.at += 1

    def whole(self):
        return self.at == 2 * len(self.rounds) - 1


def step_all(token, groups, *more):
    groups = [g for g in groups if not g.whole()]
    token, results = joint(token, *[g.job() for g in groups], *more)
    for g, r in zip(groups, results):
        g.take(r)
    return token, [r[0] for r in results[len(groups) :]]


def on_device(
    features,
    labels,
    label_mask,
    graph_sizes,
    block_index,
    block_mask,
    edge_weight,
    step_count,
    branch_weight,
    branch_moment,
    concat_weight,
    concat_moment,
    input_weight,
    input_moment,
    input_second,
    head_weight,
    head_moment,
    head_second,
):
    core = lax.axis_index("branch")
    place = lax.axis_index("dp")
    layers = branch_weight.shape[0]
    labs = labels.shape[0]
    core_arg = core.astype(jnp.int32).reshape(1)
    features_t = features.T
    sides = sides_of(core, place)
    side = sides[0]

    own = cast_weights(branch_weight, concat_weight)
    other = across_cores(own)
    adj, hid = build(block_index, block_mask, graph_sizes, edge_weight, features_t, input_weight)
    out = forward(core_arg, side, graph_sizes, adj, hid, own, other, head_weight, labels, label_mask[None, :], layers)
    kept = layers - 1
    incats, outcats, joins = out[:kept], out[kept : 2 * kept], out[2 * kept : 3 * kept]
    send, keep, ghead, totals, gself, gagg = out[3 * kept :]
    shared = (adj, own, other)

    def back(l, *extra):
        return backward(
            core_arg, side, graph_sizes, shared, (joins[l], incats[l], outcats[l], gself, gagg), extra, layers, l
        )

    for l in reversed(range(1, layers - 1)):
        send, keep, gself, gagg, token = back(l, send, keep, totals)
    upper = Summing(send, keep, sides, totals, [WIDTH] * kept)
    send, keep, token = back(0, features_t, ghead)
    held = lax.optimization_barrier((branch_moment, concat_moment, token))
    other_moments = (across_cores(held[0]), across_cores(held[1]))
    token, _ = step_all(token, [upper])
    token, (send,) = step_all(token, [upper], ("pass", side, [send], [shaped(*send.shape)]))
    lower = Summing(send, keep, sides, None, [WIDTH, keep.shape[0] - WIDTH])
    while not upper.whole():
        token, _ = step_all(token, [upper, lower])
    totals = upper.totals
    loss_scale = 1.0 / (jnp.maximum(totals[4, 0], 1.0) * labs)
    loss = totals[0, 0] * loss_scale

    moments = (branch_moment, concat_moment, *other_moments)
    weights = (branch_weight, concat_weight)
    scale = loss_scale.reshape(1)
    theirs = (side == core).astype(jnp.int32)

    def offer(group, n):
        return ("choose", theirs, [group.mine[n], group.got[n]], [shaped(WIDTH, WIDTH)])

    kept_out = []
    ortho = []
    for n, l in enumerate(reversed(range(1, layers))):
        token, (swap,) = step_all(token, [lower], offer(upper, n))
        *kept_out, sent, token = muon(
            core_arg, side, scale, upper.mine[n], upper.got[n], across_cores(swap), moments, weights, token, kept_out, ortho, layers, l
        )
        ortho = [across_cores(sent)]
    while not lower.whole():
        token, _ = step_all(token, [lower])
    n_rest = lower.mine[1].shape[0]
    token, (swap, rest) = step_all(
        token, [], offer(lower, 0), ("gather", side, [lower.mine[1], lower.got[1]], [shaped(2 * n_rest, WIDTH)])
    )
    *kept_out, sent, token = muon(
        core_arg, side, scale, lower.mine[0], lower.got[0], across_cores(swap), moments, weights, token, kept_out, ortho, layers, 0
    )
    branch_next, concat_next = kept_out[:2]
    sent = across_cores(sent)
    steps = step_count[0].astype(F32)
    numbers = jnp.stack(
        [loss_scale, 1.0 / (1.0 - jnp.power(first_decay, steps)), 1.0 / (1.0 - jnp.power(second_decay, steps))]
    )
    *ends_out, branch_new, concat_new = adam(
        core_arg,
        numbers,
        rest,
        across_cores(rest),
        weights,
        *kept_out[2:],
        sent,
        (input_weight, input_moment, input_second),
        (head_weight, head_moment, head_second),
    )
    return (loss, branch_new, branch_next, concat_new, concat_next, *ends_out)


def solution(mesh):
    placed = (
        P("dp", None),
        P(None, "dp"),
        P("dp"),
        P("dp"),
        P("dp", None),
        P("dp", None),
        P("dp", None, None, None),
        P(),
        P(None, "branch", None, None),
        P(None, "branch", None, None),
        P(None, "branch", None),
        P(None, "branch", None),
        P(),
        P(),
        P(),
        P(),
        P(),
        P(),
    )
    return jax.shard_map(
        on_device,
        mesh=mesh,
        in_specs=placed,
        out_specs=(
            P(),
            P(None, "branch", None, None),
            P(None, "branch", None, None),
            P(None, "branch", None),
            P(None, "branch", None),
            P(),
            P(),
            P(),
            P(),
            P(),
            P(),
        ),
        check_vma=False,
    )
```

```python
import functools
import jax
import jax.numpy as jnp
from jax import lax
from jax.experimental import pallas as pl
from jax.experimental.pallas import tpu as pltpu
from jax.sharding import PartitionSpec as P

NS_STEPS = 5
WIDTH = 512
HALF = WIDTH // 2
BLK = 128
LABPAD = 128
SUB = 256

quintic_one = 3.4445
quintic_two = -4.775
quintic_three = 2.0315
norm_epsilon = 1e-06
momentum_decay = 0.95
muon_rate = 0.5
first_decay = 0.9
second_decay = 0.999
adam_epsilon = 1e-08
weight_decay = 0.01

F32 = jnp.float32
BF16 = jnp.bfloat16
MB = 1 << 20
VM = pltpu.VMEM
DMA = pltpu.SemaphoreType.DMA
WIDE = 2 * WIDTH


def nn(a, b):
    return jnp.dot(a, b, preferred_element_type=F32)


def nt(a, b):
    return lax.dot_general(a, b, (((1,), (1,)), ((), ())), preferred_element_type=F32)


def tn(a, b):
    return lax.dot_general(a, b, (((0,), (0,)), ((), ())), preferred_element_type=F32)


def vmem():
    return pl.BlockSpec(memory_space=VM)


def smem():
    return pl.BlockSpec(memory_space=pltpu.SMEM)


def anywhere():
    return pl.BlockSpec(memory_space=pl.ANY)


def in_hbm():
    return pl.BlockSpec(memory_space=pltpu.HBM)


def far(x):
    return pltpu.with_memory_space_constraint(x, pltpu.HBM)


def shaped(*shape, dtype=BF16):
    return jax.ShapeDtypeStruct(shape, dtype)


def params(limit):
    return pltpu.CompilerParams(vmem_limit_bytes=limit * MB)


def cost(us):
    return pl.CostEstimate(flops=int(us), bytes_accessed=1, transcendentals=0)


def moved(src, dst, sem):
    cp = pltpu.make_async_copy(src, dst, sem)
    cp.start()
    return cp


def picked(first, a, b, dst, sem):
    @pl.when(first)
    def _():
        pltpu.make_async_copy(a, dst, sem).start()

    @pl.when(jnp.logical_not(first))
    def _():
        pltpu.make_async_copy(b, dst, sem).start()

    return pltpu.make_async_copy(a, dst, sem)


def cast_kernel(branch_hbm, concat_hbm, out_hbm, wide, low, in_sems, out_sems):
    layers = branch_hbm.shape[0]
    loads = []
    for l in range(layers):
        loads.append((0, l, moved(branch_hbm.at[l, 0], wide.at[0, l], in_sems.at[0, l])))
        loads.append((1, l, moved(concat_hbm.at[l], wide.at[1, l], in_sems.at[1, l])))
    stores = []
    for n, l, cp in loads:
        cp.wait()
        low[n, l] = wide[n, l].astype(BF16)
        stores.append(moved(low.at[n, l], out_hbm.at[n, l], out_sems.at[n, l]))
    for cp in stores:
        cp.wait()


def cast_weights(branch_weight, concat_weight):
    layers = branch_weight.shape[0]
    shape = (2, layers, WIDTH, WIDTH)
    return pl.pallas_call(
        cast_kernel,
        in_specs=[in_hbm()] * 2,
        out_specs=in_hbm(),
        out_shape=pltpu.HBM(shape, BF16),
        scratch_shapes=[VM(shape, F32), VM(shape, BF16), DMA((2, layers)), DMA((2, layers))],
        compiler_params=params(16),
        cost_estimate=cost(4),
        name="weights",
    )(far(branch_weight), far(concat_weight))


def build_kernel(index_ref, mask_ref, size_ref, edge_ref, feat_ref, win_ref, adj_ref, hid_ref, acc_ref, win):
    step = pl.program_id(0)
    per, kb = edge_ref.shape[0], edge_ref.shape[1]

    @pl.when(step == 0)
    def _():
        win[...] = win_ref[...].astype(BF16)

    for i in range(per):
        acc_ref[...] = jnp.zeros_like(acc_ref)
        for k in range(kb):
            at = pl.multiple_of(index_ref[step * per + i, k] * BLK, BLK)
            keep = mask_ref[step * per + i, k].astype(F32)
            acc_ref[:, pl.ds(at, BLK)] += edge_ref[i, k].astype(F32) * keep
        adj_ref[i * BLK : (i + 1) * BLK, :] = acc_ref[...].astype(BF16)
    size = per * BLK
    inside = lax.broadcasted_iota(jnp.int32, (size, 1), 0) + step * size < size_ref[0]
    hidden = tn(feat_ref[...], win[...])
    hid_ref[...] = jnp.where(inside, hidden, 0.0).astype(BF16)


def build(block_index, block_mask, graph_sizes, edge_weight, features_t, input_weight):
    nb, kb = block_index.shape
    feats, rows = features_t.shape
    per = 4 if nb % 4 == 0 else 2
    return pl.pallas_call(
        build_kernel,
        grid=(nb // per,),
        in_specs=[
            smem(),
            smem(),
            smem(),
            pl.BlockSpec((per, kb, BLK, BLK), lambda i: (i, 0, 0, 0)),
            pl.BlockSpec((feats, per * BLK), lambda i: (0, i)),
            pl.BlockSpec((feats, WIDTH), lambda i: (0, 0)),
        ],
        out_specs=[
            pl.BlockSpec((per * BLK, rows), lambda i: (i, 0)),
            pl.BlockSpec((per * BLK, WIDTH), lambda i: (i, 0)),
        ],
        out_shape=[pltpu.HBM((rows, rows), BF16), pltpu.HBM((rows, WIDTH), BF16)],
        scratch_shapes=[VM((BLK, rows), F32), VM((feats, WIDTH), BF16)],
        compiler_params=params(32),
        cost_estimate=cost(8),
        name="adjacency",
    )(block_index, block_mask, graph_sizes, far(edge_weight), far(features_t), far(input_weight))


def inside_of(size_ref, at, tile):
    return lax.broadcasted_iota(jnp.int32, (tile, 1), 0) + at < size_ref[0]


def joined_back(joined, grad, inside):
    grad = jnp.where(inside, grad, 0.0)
    sigma = jax.nn.sigmoid(joined)
    activated = joined * sigma
    inverse = lax.rsqrt(jnp.sum(activated * activated, 1, keepdims=True) + norm_epsilon)
    along = jnp.sum(activated * grad, 1, keepdims=True)
    grad_act = inverse * grad - (inverse * inverse * inverse * along) * activated
    return (grad_act * sigma * (1.0 + joined * (1.0 - sigma))).astype(BF16)


def weight_grads(core, low, incat, outcat, gj, gcat, send_ref, keep_ref):
    mine = pl.ds(pl.multiple_of(core * WIDTH, WIDTH), WIDTH)
    branch = tn(incat[:, mine], gcat[:, mine])
    concat = tn(outcat[:, mine], gj[...])
    send_ref[...] = jnp.where(low, concat, branch).astype(BF16)
    keep_ref[...] = jnp.where(low, branch, concat)


def layer_tile_back(joined, grad, inside, c_ref, w1_ref, rows, gj, gcat, gagg):
    g = joined_back(joined, grad, inside)
    gj[rows, :] = g
    both = nt(g, c_ref[...]).astype(BF16)
    gcat[rows, :] = both
    gagg[rows, :] = nt(both[:, WIDTH:], w1_ref[...]).astype(BF16)


def forward_kernel(
    layers,
    tile,
    core_ref,
    side_ref,
    size_ref,
    adj_hbm,
    hid_hbm,
    own_hbm,
    other_hbm,
    head_ref,
    labels_ref,
    mask_ref,
    *refs,
):
    kept = layers - 1
    in_out = refs[:kept]
    out_out = refs[kept : 2 * kept]
    join_out = refs[2 * kept : 3 * kept]
    send_hbm, keep_hbm, ghead_hbm, totals_hbm, gself_hbm, gagg_hbm = refs[3 * kept : 3 * kept + 6]
    refs = refs[3 * kept + 6 :]
    incat = [refs[l % 2] for l in range(layers)]
    outcat = [refs[2 + l % 2] for l in range(layers)]
    adj, w, c, joined, last, head, gl, glb, gj, send, keep, ghead_ref, totals_ref, sems, out_sems, end_sems = refs[4:]
    gcat, gagg = adj.at[:, pl.ds(0, WIDE)], adj.at[:, pl.ds(WIDE, WIDTH)]
    core = core_ref[0]
    other = 1 - core
    rows_total = adj.shape[0]
    tiles = rows_total // tile
    own_rows = pl.ds(pl.multiple_of(core * WIDTH, WIDTH), WIDTH)
    other_rows = pl.ds(pl.multiple_of(other * WIDTH, WIDTH), WIDTH)

    hid_cp = moved(hid_hbm, incat[0].at[:, pl.ds(0, WIDTH)], sems.at[0])
    adj_cps = [
        moved(adj_hbm.at[pl.ds(t * tile, tile)], adj.at[pl.ds(t * tile, tile)], sems.at[1 + t]) for t in range(tiles)
    ]
    weight_cps = []
    for l in range(layers):
        base = 1 + tiles + 4 * l
        weight_cps.append(
            [
                moved(own_hbm.at[0, l], w.at[l, core], sems.at[base]),
                moved(other_hbm.at[0, l], w.at[l, other], sems.at[base + 1]),
                moved(own_hbm.at[1, l], c.at[l, own_rows, :], sems.at[base + 2]),
                moved(other_hbm.at[1, l], c.at[l, other_rows, :], sems.at[base + 3]),
            ]
        )
    labs, width = head_ref.shape
    head[...] = jnp.zeros_like(head)
    head[0:labs, :] = head_ref[...].astype(BF16)
    lane = lax.broadcasted_iota(jnp.int32, (1, rows_total), 1)
    counted_all = jnp.where(lane < size_ref[0], mask_ref[...].astype(F32), 0.0)
    hid_cp.wait()
    stores = []
    for l in range(layers):
        src, dst, jo = incat[l], outcat[l], joined.at[l % 2]
        if l >= 2:
            stores[l - 2][1].wait()
            stores[l - 2][2].wait()
        for t in range(tiles):
            rows = pl.ds(t * tile, tile)
            if l == 0:
                adj_cps[t].wait()
            neigh = nn(adj[rows, :], src[:, 0:WIDTH]).astype(BF16)
            src[rows, WIDTH:] = neigh
            if t == 0:
                for cp in weight_cps[l]:
                    cp.wait()
            dst[rows, 0:WIDTH] = nn(src[rows, 0:WIDTH], w[l, 0]).astype(BF16)
            dst[rows, WIDTH:] = nn(neigh, w[l, 1]).astype(BF16)
            for u in range(0, tile, SUB):
                part = pl.ds(t * tile + u, SUB)
                j = nn(dst[part, :], c[l])
                jo[part, :] = j
                activated = j * jax.nn.sigmoid(j)
                inverse = lax.rsqrt(jnp.sum(activated * activated, 1, keepdims=True) + norm_epsilon)
                inverse = jnp.where(inside_of(size_ref, t * tile + u, SUB), inverse, 0.0)
                hidden = (activated * inverse).astype(BF16)
                if 1 <= l < layers - 1 and t == 0 and u == 0:
                    stores[l - 1][0].wait()
                if l + 1 < layers:
                    incat[l + 1][part, 0:WIDTH] = hidden
                else:
                    last[part, :] = hidden
        if l < kept:
            pairs = ((src, in_out[l]), (dst, out_out[l]), (jo, join_out[l]))
            stores.append([moved(a, b, out_sems.at[3 * l + n]) for n, (a, b) in enumerate(pairs)])

    gl[...] = jnp.zeros_like(gl)
    loss = jnp.zeros((1, 1), F32)
    for t in range(tiles):
        rows = pl.ds(t * tile, tile)
        lanes = slice(t * tile, (t + 1) * tile)
        logits = nt(head[...], last[rows, :])[:labs]
        targets = labels_ref[:, lanes].astype(F32)
        counted = counted_all[:, lanes]
        small = jnp.exp(-jnp.abs(logits))
        ratio = 1.0 / (1.0 + small)
        sigma = jnp.where(logits >= 0.0, ratio, small * ratio)
        soft = jnp.maximum(logits, 0.0) + jnp.log1p(small)
        per_node = jnp.sum(soft - targets * logits, 0, keepdims=True)
        loss = loss + jnp.sum(per_node * counted, 1, keepdims=True)
        gl[0:labs, lanes] = counted * (sigma - targets)
    glb[...] = gl[...].astype(BF16)
    totals_ref[0:4, :] = jnp.broadcast_to(loss, (4, 128))
    totals_ref[4:8, :] = jnp.broadcast_to(jnp.sum(counted_all, 1, keepdims=True), (4, 128))
    ghead = nn(glb[...], last[:, pl.ds(pl.multiple_of(core * HALF, HALF), HALF)])
    mid = LABPAD // 2
    ghead_ref[:, 0:HALF] = ghead[:mid]
    ghead_ref[:, HALF:] = ghead[mid:]

    l = layers - 1
    jo = joined.at[l % 2]
    for t in range(tiles):
        rows = pl.ds(t * tile, tile)
        grad = tn(glb[:, t * tile : (t + 1) * tile], head[...])
        inside = inside_of(size_ref, t * tile, tile)
        layer_tile_back(jo[rows, :], grad, inside, c.at[l], w.at[l, 1], rows, gj, gcat, gagg)
    outs = [
        moved(gcat.at[:, pl.ds(0, WIDTH)], gself_hbm, end_sems.at[0]),
        moved(gagg, gagg_hbm, end_sems.at[1]),
        moved(ghead_ref, ghead_hbm, end_sems.at[4]),
        moved(totals_ref, totals_hbm, end_sems.at[5]),
    ]
    weight_grads(core, side_ref[0] == 0, incat[l], outcat[l], gj, gcat, send, keep)
    outs += [moved(send, send_hbm, end_sems.at[2]), moved(keep, keep_hbm, end_sems.at[3])]
    for cp in outs:
        cp.wait()
    for n, group in enumerate(stores):
        for cp in group if n + 2 >= layers else []:
            cp.wait()


def forward(core, side, size, adj, hid, own, other, head, labels, mask, layers):
    rows = adj.shape[0]
    kept = layers - 1
    tile = rows // 2
    wide = pltpu.HBM((rows, WIDE), BF16)
    out_shape = (
        [wide] * (2 * kept)
        + [pltpu.HBM((rows, WIDTH), F32)] * kept
        + [
            pltpu.HBM((WIDTH, WIDTH), BF16),
            pltpu.HBM((WIDTH, WIDTH), F32),
            pltpu.HBM((LABPAD // 2, WIDTH), F32),
            pltpu.HBM((8, BLK), F32),
            pltpu.HBM((rows, WIDTH), BF16),
            pltpu.HBM((rows, WIDTH), BF16),
        ]
    )
    return pl.pallas_call(
        functools.partial(forward_kernel, layers, tile),
        in_specs=[smem()] * 3 + [in_hbm()] * 4 + [vmem()] * 3,
        out_specs=[in_hbm()] * (3 * kept + 6),
        out_shape=out_shape,
        scratch_shapes=[VM((rows, WIDE), BF16)] * 4
        + [
            VM((rows, rows), BF16),
            VM((layers, 2, WIDTH, WIDTH), BF16),
            VM((layers, WIDE, WIDTH), BF16),
            VM((2, rows, WIDTH), F32),
            VM((rows, WIDTH), BF16),
            VM((LABPAD, WIDTH), BF16),
            VM((LABPAD, rows), F32),
            VM((LABPAD, rows), BF16),
            VM((rows, WIDTH), BF16),
            VM((WIDTH, WIDTH), BF16),
            VM((WIDTH, WIDTH), F32),
            VM((LABPAD // 2, WIDTH), F32),
            VM((8, BLK), F32),
            DMA((1 + rows // tile + 4 * layers,)),
            DMA((3 * kept,)),
            DMA((6,)),
        ],
        compiler_params=params(42),
        cost_estimate=cost(30),
        name="forward",
    )(core, side, size, far(adj), far(hid), far(own), far(other), head, labels, mask)


def backward_kernel(layers, l, tile, core_ref, side_ref, size_ref, *refs):
    adj_hbm, own_hbm, other_hbm, joined_hbm, incat_hbm, outcat_hbm, gself_hbm, gagg_hbm = refs[:8]
    refs = refs[8:]
    if l:
        send_hbm, keep_hbm, totals_hbm, send_ref, keep_ref, gself_out, gagg_out, token_ref = refs[:8]
        refs = refs[8:]
    else:
        feat_hbm, ghead_hbm, send_ref, keep_ref, token_ref = refs[:5]
        w0, feat, first_grad, rest, last_sems = refs[-5:]
        refs = refs[5:-5]
    adj, wself, w1, c, joined, incat, outcat, gj, gcat, gself_in, gagg_in, gagg, totals, sems, adj_sems, join_sems = refs
    token_ref[...] = jnp.zeros_like(token_ref)
    core = core_ref[0]
    other = 1 - core
    low = side_ref[0] == 0
    tiles = adj.shape[0] // tile
    first = core == 0

    def load_tile(t):
        rows = pl.ds(t * tile, tile)
        return (
            moved(adj_hbm.at[:, rows], adj.at[:, rows], adj_sems.at[t]),
            moved(joined_hbm.at[rows], joined.at[rows], join_sems.at[t]),
        )

    early = [
        moved(gagg_hbm, gagg_in, sems.at[6]),
        picked(first, own_hbm.at[0, l + 1], other_hbm.at[0, l + 1], wself, sems.at[0]),
        moved(gself_hbm, gself_in, sems.at[7]),
    ]
    tile_cps = [load_tile(0)]
    own_rows = pl.ds(pl.multiple_of(core * WIDTH, WIDTH), WIDTH)
    other_rows = pl.ds(pl.multiple_of(other * WIDTH, WIDTH), WIDTH)
    weight_cps = [
        picked(first, other_hbm.at[0, l], own_hbm.at[0, l], w1, sems.at[1]),
        moved(own_hbm.at[1, l], c.at[own_rows, :], sems.at[2]),
        moved(other_hbm.at[1, l], c.at[other_rows, :], sems.at[3]),
    ]
    if l == 1:
        early.append(moved(totals_hbm, totals, sems.at[12]))
    for cp in early:
        cp.wait()
    if l == 1:
        put_totals(send_ref, keep_ref.shape[0], totals[...])
    done = keep_hbm.shape[0] if l else 0
    late, outs = [], []
    for t in range(tiles):
        rows = pl.ds(t * tile, tile)
        tile_cps[t][0].wait()
        if t + 1 < tiles:
            tile_cps.append(load_tile(t + 1))
        if t == 0:
            late += [moved(incat_hbm, incat, sems.at[4]), moved(outcat_hbm, outcat, sems.at[5])]
            if l:
                late += [
                    moved(send_hbm.at[pl.ds(0, done)], send_ref.at[pl.ds(0, done)], sems.at[8]),
                    moved(keep_hbm, keep_ref.at[pl.ds(0, done)], sems.at[9]),
                ]
            else:
                late += [
                    picked(first, own_hbm.at[0, 0], other_hbm.at[0, 0], w0, last_sems.at[0]),
                    moved(feat_hbm, feat, last_sems.at[1]),
                ]
        grad = tn(adj[:, rows], gagg_in[...]) + nt(gself_in[rows, :], wself[...])
        tile_cps[t][1].wait()
        if t == 0:
            for cp in weight_cps:
                cp.wait()
        inside = inside_of(size_ref, t * tile, tile)
        layer_tile_back(joined[rows, :], grad, inside, c, w1, rows, gj, gcat, gagg)
    if l:
        outs = [
            moved(gcat.at[:, pl.ds(0, WIDTH)], gself_out, sems.at[10]),
            moved(gagg, gagg_out, sems.at[11]),
        ]
    for cp in late:
        cp.wait()
    here = slice(done, done + WIDTH)
    weight_grads(core, low, incat, outcat, gj, gcat, send_ref.at[here], keep_ref.at[here])
    for cp in outs:
        cp.wait()
    if l:
        return
    feats = feat.shape[0]
    mid = LABPAD // 2
    tall = pl.cdiv(feats, BLK) * BLK // 2
    rest[...] = jnp.zeros_like(rest)
    head_cp = moved(ghead_hbm, rest.at[pl.ds(tall, mid)], last_sems.at[2])
    mine = pl.ds(pl.multiple_of(core * HALF, HALF), HALF)
    for t in range(tiles):
        rows = pl.ds(t * tile, tile)
        grad = tn(adj[:, rows], gagg[:, mine]) + nt(gcat[rows, 0:WIDTH], w0[mine, :])
        grad = jnp.where(inside_of(size_ref, t * tile, tile), grad, 0.0)
        first_grad[rows, :] = grad.astype(BF16)
    grad = nn(feat[...], first_grad[...])
    rest[0:tall, 0:HALF] = grad[0:tall]
    rest[0 : feats - tall, HALF:] = grad[tall:]
    head_cp.wait()
    half = rest.shape[0] // 2
    upper, lower = rest[0:half, :], rest[half:, :]
    send_ref[WIDTH:, :] = jnp.where(low, lower, upper).astype(BF16)
    keep_ref[WIDTH:, :] = jnp.where(low, upper, lower)


def backward(core, side, size, shared, kept, extra, layers, l):
    rows = shared[0].shape[0]
    tile = rows // 2
    scratch = [
        VM((rows, rows), BF16),
        VM((WIDTH, WIDTH), BF16),
        VM((WIDTH, WIDTH), BF16),
        VM((WIDE, WIDTH), BF16),
        VM((rows, WIDTH), F32),
        VM((rows, WIDE), BF16),
        VM((rows, WIDE), BF16),
        VM((rows, WIDTH), BF16),
        VM((rows, WIDE), BF16),
        VM((rows, WIDTH), BF16),
        VM((rows, WIDTH), BF16),
        VM((rows, WIDTH), BF16),
        VM((8, BLK), F32),
        DMA((13,)),
        DMA((rows // tile,)),
        DMA((rows // tile,)),
    ]
    token = shaped(8, BLK, dtype=F32)
    if l:
        tall = WIDTH * (layers - l)
        more = EXTRA if l == 1 else 0
        hbm = pltpu.HBM((rows, WIDTH), BF16)
        out_shape = [shaped(tall + more, WIDTH), shaped(tall, WIDTH, dtype=F32), hbm, hbm, token]
        out_specs = [vmem()] * 2 + [in_hbm()] * 2 + [vmem()]
    else:
        feats = extra[0].shape[0]
        tall = pl.cdiv(feats, BLK) * BLK // 2
        unit = 8 * lax.axis_size("dp")
        out = pl.cdiv(WIDTH + (tall + LABPAD // 2 + 1) // 2, unit) * unit
        rest = 2 * (out - WIDTH)
        out_shape = [shaped(out, WIDTH), shaped(out, WIDTH, dtype=F32), token]
        out_specs = [vmem()] * 3
        scratch += [
            VM((WIDTH, WIDTH), BF16),
            VM((feats, rows), BF16),
            VM((rows, HALF), BF16),
            VM((rest, WIDTH), F32),
            DMA((3,)),
        ]
    args = [far(x) for x in (*shared, *kept, *extra)]
    return pl.pallas_call(
        functools.partial(backward_kernel, layers, l, tile),
        in_specs=[smem()] * 3 + [in_hbm()] * len(args),
        out_specs=out_specs,
        out_shape=out_shape,
        scratch_shapes=scratch,
        compiler_params=params(36),
        cost_estimate=cost(15),
        name=f"backward{l}",
    )(core, side, size, *args)


def muon_kernel(
    layers,
    l,
    core_ref,
    side_ref,
    scale_ref,
    mine_hbm,
    got_hbm,
    swap_hbm,
    mb_hbm,
    mc_hbm,
    other_mb_hbm,
    other_mc_hbm,
    wb_hbm,
    wc_hbm,
    token_in,
    *refs,
):
    above = l < layers - 1
    if above:
        ortho_ref = refs[4]
        refs = refs[5:]
    bnext_hbm, cnext_hbm, bnew_hbm, cnew_hbm, sent_out, token_ref = refs[:6]
    gb, gc, gs, mb, mc, ms, wk, wa, x, sems = refs[6:]
    token_ref[...] = jnp.zeros_like(token_ref)
    first = core_ref[0] == 0
    low_side = side_ref[0] == 0
    scale = scale_ref[0]
    cps = [
        picked(low_side, mine_hbm, got_hbm, gb, sems.at[0]),
        picked(low_side, got_hbm, mine_hbm, gc, sems.at[1]),
        moved(mb_hbm.at[l, 0], mb, sems.at[2]),
        moved(mc_hbm.at[l], mc, sems.at[3]),
        moved(swap_hbm, gs, sems.at[4]),
        picked(first, other_mc_hbm.at[l], other_mb_hbm.at[l, 0], ms, sems.at[5]),
    ]
    late = picked(first, wc_hbm.at[l], wb_hbm.at[l, 0], wk, sems.at[6])
    if above:
        above_cp = picked(first, wb_hbm.at[l + 1, 0], wc_hbm.at[l + 1], wa, sems.at[10])
    for cp in cps:
        cp.wait()
    mb[...] = momentum_decay * mb[...] + scale * gb[...].astype(F32)
    mc[...] = momentum_decay * mc[...] + scale * gc[...].astype(F32)
    stores = [moved(mb, bnext_hbm.at[l, 0], sems.at[7]), moved(mc, cnext_hbm.at[l], sems.at[8])]
    ms[...] = momentum_decay * ms[...] + scale * gs[...].astype(F32)
    if above:
        above_cp.wait()
        other_gain = jnp.where(first, 1.0, 2.0**0.5)
        wa[...] = wa[...] - muon_rate * (other_gain * ortho_ref[...].astype(F32) + weight_decay * wa[...])
        stores.append(picked_out(first, wa, bnew_hbm.at[l + 1, 0], cnew_hbm.at[l + 1], sems.at[11]))

    a = jnp.where(first, mc[...], mb[...])
    b = ms[...]
    na, nb = jnp.sum(a * a), jnp.sum(b * b)
    link = jnp.where(first, 1.0, 0.0)
    x[0:WIDTH, :] = a * (1.0 / (jnp.sqrt(jnp.full((1, 1), na + link * nb, F32)) + 1e-07))
    x[WIDTH:, :] = b * (1.0 / (jnp.sqrt(jnp.full((1, 1), nb + link * na, F32)) + 1e-07))

    def sweep(blocks, shift):
        zero = quintic_one + quintic_two * shift + quintic_three * shift * shift
        slope = quintic_two + 2.0 * quintic_three * shift
        low = [x[block, :].astype(BF16) for block in blocks]
        grams = []
        for v in low:
            left, right = v[:, :HALF], v[:, HALF:]
            grams.append((tn(left, left), tn(left, right), tn(right, right)))
        if shift:
            at = lax.broadcasted_iota(jnp.int32, (HALF, HALF), 0) == lax.broadcasted_iota(jnp.int32, (HALF, HALF), 1)
            eye = jnp.where(at, shift, 0.0)
            grams = [(g - eye, h, k - eye) for g, h, k in grams]
        polys = []
        for gram in grams:
            corner, side, tail = [g.astype(BF16) for g in gram]
            top = jnp.concatenate([corner, side], 1)
            bottom = jnp.concatenate([side.T, tail], 1)
            squares = (nt(top, top), nt(top, bottom), nt(bottom, bottom))
            corner, side, tail = [(slope * g + quintic_three * q).astype(BF16) for g, q in zip(gram, squares)]
            top = jnp.concatenate([corner, side], 1)
            polys.append(jnp.concatenate([top, jnp.concatenate([side.T, tail], 1)], 0))
        for block, v, p in zip(blocks, low, polys):
            x[block, :] = zero * x[block, :] + nn(v, p)

    def sweeps(blocks):
        @pl.loop(0, NS_STEPS - 1)
        def _(step):
            sweep(blocks, 0.0)

        sweep(blocks, 0.75)

    @pl.when(first)
    def _():
        sweeps([slice(0, WIDE)])

    @pl.when(jnp.logical_not(first))
    def _():
        sweeps([slice(0, WIDTH), slice(WIDTH, WIDE)])

    sent_out[...] = x[WIDTH:, :].astype(BF16)
    late.wait()
    gain = jnp.where(first, 2.0**0.5, 1.0)
    wk[...] = wk[...] - muon_rate * (gain * x[0:WIDTH, :] + weight_decay * wk[...])
    stores.append(picked_out(first, wk, cnew_hbm.at[l], bnew_hbm.at[l, 0], sems.at[9]))
    for cp in stores:
        cp.wait()


def picked_out(first, src, a, b, sem):
    @pl.when(first)
    def _():
        pltpu.make_async_copy(src, a, sem).start()

    @pl.when(jnp.logical_not(first))
    def _():
        pltpu.make_async_copy(src, b, sem).start()

    return pltpu.make_async_copy(src, a, sem)


def muon(core, side, scale, mine, got, swap, moments, weights, token, kept, ortho, layers, l):
    square = VM((WIDTH, WIDTH), F32)
    low = VM((WIDTH, WIDTH), BF16)
    args = [core, side, scale, mine, got, swap, *[far(x) for x in (*moments, *weights)], token, *kept, *ortho]
    return pl.pallas_call(
        functools.partial(muon_kernel, layers, l),
        in_specs=[smem()] * 3 + [anywhere()] * 3 + [in_hbm()] * 6 + [anywhere()] + [in_hbm()] * len(kept) + [vmem()] * len(ortho),
        out_specs=[in_hbm()] * 4 + [vmem()] * 2,
        out_shape=[
            pltpu.HBM((layers, 1, WIDTH, WIDTH), F32),
            pltpu.HBM((layers, WIDTH, WIDTH), F32),
            pltpu.HBM((layers, 1, WIDTH, WIDTH), F32),
            pltpu.HBM((layers, WIDTH, WIDTH), F32),
            shaped(WIDTH, WIDTH),
            shaped(8, BLK, dtype=F32),
        ],
        input_output_aliases={13 + n: n for n in range(len(kept))},
        scratch_shapes=[low, low, low, square, square, square, square, square, VM((WIDE, WIDTH), F32), DMA((12,))],
        compiler_params=params(24),
        cost_estimate=cost(13),
        name="muon",
    )(*args)


def finish_kernel(where, core_ref, wb_hbm, wc_hbm, bnew_in, cnew_in, token_in, *refs):
    count = len(where)
    orthos = refs[:count]
    bnew_hbm, cnew_hbm, token_ref, wk, sems = refs[count:]
    token_ref[...] = jnp.zeros_like(token_ref)
    first = core_ref[0] == 0
    loads = [picked(first, wb_hbm.at[l, 0], wc_hbm.at[l], wk.at[n], sems.at[n]) for n, l in enumerate(where)]
    gain = jnp.where(first, 1.0, 2.0**0.5)
    stores = []
    for n, l in enumerate(where):
        loads[n].wait()
        w = wk[n]
        wk[n] = w - muon_rate * (gain * orthos[n][...].astype(F32) + weight_decay * w)
        stores.append(picked_out(first, wk.at[n], bnew_hbm.at[l, 0], cnew_hbm.at[l], sems.at[count + n]))
    for cp in stores:
        cp.wait()


def finish(core, weights, bnew, cnew, token, orthos, where, layers):
    count = len(where)
    return pl.pallas_call(
        functools.partial(finish_kernel, where),
        in_specs=[smem()] + [in_hbm()] * 4 + [anywhere()] + [vmem()] * count,
        out_specs=[in_hbm()] * 2 + [vmem()],
        out_shape=[
            pltpu.HBM((layers, 1, WIDTH, WIDTH), F32),
            pltpu.HBM((layers, WIDTH, WIDTH), F32),
            shaped(8, BLK, dtype=F32),
        ],
        input_output_aliases={3: 0, 4: 1},
        scratch_shapes=[VM((count, WIDTH, WIDTH), F32), DMA((2 * count,))],
        compiler_params=params(16),
        cost_estimate=cost(3),
        name="finish",
    )(core, *[far(x) for x in weights], bnew, cnew, token, *orthos)


def adam_step(weight, moment, second, grad, rate, first_fix, second_fix):
    moment = first_decay * moment + (1.0 - first_decay) * grad
    second = second_decay * second + (1.0 - second_decay) * grad * grad
    corrected = (moment * first_fix) / (jnp.sqrt(second * second_fix) + adam_epsilon)
    return (weight - rate * (corrected + weight_decay * weight), moment, second)


def adam_kernel(core_ref, numbers_ref, own_ref, other_ref, token_in, *refs):
    refs[12][...] = jnp.zeros_like(refs[12])
    grad = refs[13]
    scale, first_fix, second_fix = numbers_ref[0], numbers_ref[1], numbers_ref[2]
    tall = grad.shape[0] // 2
    mid = LABPAD // 2
    core = core_ref[0]
    for ref, at in ((own_ref, core), (other_ref, 1 - core)):
        lanes = pl.ds(pl.multiple_of(at * HALF, HALF), HALF)
        grad[0:tall, lanes] = ref[0:tall, 0:HALF].astype(F32)
        grad[tall : 2 * tall, lanes] = ref[0:tall, HALF:].astype(F32)
    feats = refs[0].shape[0]
    outs = adam_step(refs[0][...], refs[1][...], refs[2][...], scale * grad[0:feats, :], 0.02, first_fix, second_fix)
    for ref, value in zip(refs[6:9], outs):
        ref[...] = value
    for ref, at in ((own_ref, core), (other_ref, 1 - core)):
        lanes = pl.ds(pl.multiple_of(at * HALF, HALF), HALF)
        grad[0:mid, lanes] = ref[tall : tall + mid, 0:HALF].astype(F32)
        grad[mid:LABPAD, lanes] = ref[tall : tall + mid, HALF:].astype(F32)
    labs = refs[3].shape[0]
    outs = adam_step(refs[3][...], refs[4][...], refs[5][...], scale * grad[0:labs, :], 0.5, first_fix, second_fix)
    for ref, value in zip(refs[9:12], outs):
        ref[...] = value


def adam(core, numbers, own, other, token, inputs, heads):
    tall = pl.cdiv(inputs[0].shape[0], BLK) * BLK // 2
    shapes = [shaped(*x.shape, dtype=F32) for x in (*inputs, *heads)] + [shaped(8, BLK, dtype=F32)]
    return pl.pallas_call(
        adam_kernel,
        in_specs=[smem(), smem()] + [vmem()] * 2 + [anywhere()] + [vmem()] * 6,
        out_specs=[vmem()] * 7,
        out_shape=shapes,
        scratch_shapes=[VM((2 * tall, WIDTH), F32)],
        compiler_params=params(24),
        cost_estimate=cost(4),
        name="adam",
    )(core, numbers, own, other, token, *inputs, *heads)


def across_cores(x):
    return lax.ppermute(x, "branch", [(0, 1), (1, 0)])


def rounds():
    bits = lax.axis_size("dp").bit_length() - 1
    first = [(b,) for b in range(min(bits, 2))] + [tuple(range(b, min(b + 2, bits))) for b in range(2, bits, 2)]
    second = first[:]
    if bits >= 2:
        second[0], second[1] = first[1], first[0]
    return list(zip(first, second))


def mask_of(bits, m):
    return sum(1 << b for n, b in enumerate(bits) if m >> n & 1)


def paired(x, both, m):
    pairs = [(i * 2 + c, (i ^ mask_of(both[c], m)) * 2 + c) for i in range(lax.axis_size("dp")) for c in range(2)]
    return lax.ppermute(x, ("dp", "branch"), pairs)


def sides_of(core, place):
    def index(bits):
        return sum(((place >> b) & 1) << n for n, b in enumerate(bits))

    return [jnp.where(core == 0, index(a), index(b)).astype(jnp.int32).reshape(1) for a, b in rounds()]


EXTRA = 16


def put_totals(send_ref, at, totals):
    high = totals.astype(BF16)
    left = totals - high.astype(F32)
    mid = left.astype(BF16)
    low = (left - mid.astype(F32)).astype(BF16)
    send_ref[at : at + EXTRA, 0:BLK] = jnp.concatenate([high, high], 0)
    send_ref[at : at + EXTRA, BLK : 2 * BLK] = jnp.concatenate([mid, mid], 0)
    send_ref[at : at + EXTRA, 2 * BLK : 3 * BLK] = jnp.concatenate([low, low], 0)
    send_ref[at : at + EXTRA, 3 * BLK :] = jnp.zeros((EXTRA, BLK), BF16)


def get_totals(got_ref, at):
    rows = got_ref[at : at + EXTRA, :].astype(F32)
    return (rows[0:8, 0:BLK] + rows[0:8, BLK : 2 * BLK]) + rows[0:8, 2 * BLK : 3 * BLK]


def scatter_step(ins, outs, more):
    side_ref, keep_ref = ins[:2]
    gots = ins[2 : len(ins) - more]
    n = keep_ref.shape[0]
    if more:
        totals = ins[-1][...]
        for got in gots:
            totals = totals + get_totals(got, n)
        outs[-1][...] = totals
        outs = outs[:-1]

    def summed(rows):
        value = keep_ref[rows, :]
        for got in gots:
            value = value + got[rows, :].astype(F32)
        return value

    if len(outs) == 1:
        outs[0][...] = summed(slice(0, n)).astype(BF16)
        return
    parts = len(outs)
    size = n // parts
    side = side_ref[0]

    def give(place):
        for m in range(1, parts):
            at = (place ^ m) * size
            outs[m - 1][0:size, :] = summed(slice(at, at + size)).astype(BF16)
        outs[-1][...] = summed(slice(place * size, place * size + size))

    for place in range(parts):
        pl.when(side == place)(functools.partial(give, place))
    if more:
        for m in range(1, parts):
            put_totals(outs[m - 1], size, totals)


def gather_step(ins, outs):
    side_ref, blocks = ins[0], ins[1:]
    n = blocks[0].shape[0]
    parts = len(blocks)

    def join(place):
        at = 0
        for ref in outs:
            done = 0
            while done < ref.shape[0]:
                block, inner = (at + done) // n, (at + done) % n
                size = min(n - inner, ref.shape[0] - done)
                ref[done : done + size, :] = blocks[block ^ place][inner : inner + size, :]
                done += size
            at += ref.shape[0]

    for place in range(parts):
        pl.when(side_ref[0] == place)(functools.partial(join, place))


def choose_step(ins, outs):
    flag_ref, mine_ref, got_ref = ins

    @pl.when(flag_ref[0] != 0)
    def _():
        outs[0][...] = mine_ref[...]

    @pl.when(flag_ref[0] == 0)
    def _():
        outs[0][...] = got_ref[...]


def pass_step(ins, outs):
    outs[0][...] = ins[1][...]


STEPS = {
    "scatter": lambda ins, outs: scatter_step(ins, outs, 0),
    "scatter_more": lambda ins, outs: scatter_step(ins, outs, 1),
    "gather": gather_step,
    "choose": choose_step,
    "pass": pass_step,
}


def joint_kernel(plan, waits, token_in, *refs):
    refs = refs[waits:]
    ins_total = sum(n for _, n, _ in plan)
    ins, outs = refs[:ins_total], refs[ins_total:]
    outs[-1][...] = jnp.zeros_like(outs[-1])
    for kind, n_in, n_out in plan:
        STEPS[kind](ins[:n_in], outs[:n_out])
        ins, outs = ins[n_in:], outs[n_out:]


def joint(token, held, *jobs):
    plan = [(kind, 1 + len(arrays), len(shapes)) for kind, _, arrays, shapes in jobs]
    in_specs, args, out_shape = [anywhere()] * (1 + len(held)), [token, *[far(x) for x in held]], []
    for _, side, arrays, shapes in jobs:
        in_specs += [smem()] + [vmem()] * len(arrays)
        args += [side, *arrays]
        out_shape += shapes
    out_shape.append(shaped(8, BLK, dtype=F32))
    outs = pl.pallas_call(
        functools.partial(joint_kernel, plan, len(held)),
        in_specs=in_specs,
        out_specs=[vmem()] * len(out_shape),
        out_shape=out_shape,
        compiler_params=params(8),
        cost_estimate=cost(0.5),
        name="step",
    )(*args)
    results = []
    for _, _, _, shapes in jobs:
        results.append(outs[: len(shapes)])
        outs = outs[len(shapes) :]
    return outs[0], results


class Summing:
    def __init__(self, send, keep, sides, totals, sizes):
        self.sends, self.keep, self.sides, self.totals, self.sizes = [send], keep, sides, totals, sizes
        self.rounds = rounds()
        self.at = 0

    def exchange(self, which, blocks):
        return [paired(x, self.rounds[which], m + 1) for m, x in enumerate(blocks)]

    def partners(self, which):
        return (1 << len(self.rounds[which][0])) - 1

    def job(self):
        count = len(self.rounds)
        at = self.at
        if at < count:
            gots = self.exchange(at, self.sends)
            n = self.keep.shape[0]
            arrays, shapes, side = [self.keep, *gots], [shaped(n, WIDTH)], self.sides[0]
            if at < count - 1:
                others = self.partners(at + 1)
                size = n // (others + 1)
                extra = 0 if self.totals is None else EXTRA
                shapes = [shaped(size + extra, WIDTH)] * others + [shaped(size, WIDTH, dtype=F32)]
                side = self.sides[at + 1]
            if self.totals is None:
                return "scatter", side, arrays, shapes
            return "scatter_more", side, [*arrays, self.totals], [*shapes, shaped(8, BLK, dtype=F32)]
        which = 2 * count - 1 - at
        others = self.partners(which)
        gots = self.exchange(which, [self.mine] * others)
        sizes = self.sizes if which == 1 else [(others + 1) * self.mine.shape[0]]
        return "gather", self.sides[which], [self.mine, *gots], [shaped(n, WIDTH) for n in sizes]

    def take(self, results):
        count = len(self.rounds)
        if self.at < count:
            if self.totals is not None:
                *results, self.totals = results
            if self.at < count - 1:
                *self.sends, self.keep = results
            else:
                self.mine = results[0]
        else:
            self.mine = results[0]
        if self.at == 2 * count - 2:
            self.mine = results
            self.got = [self.exchange(0, [part])[0] for part in results]
        self.at += 1

    def whole(self):
        return self.at == 2 * len(self.rounds) - 1


def step_all(token, groups, *more, held=()):
    groups = [g for g in groups if not g.whole()]
    token, results = joint(token, held, *[g.job() for g in groups], *more)
    for g, r in zip(groups, results):
        g.take(r)
    return token, [r[0] for r in results[len(groups) :]]


def on_device(
    features,
    labels,
    label_mask,
    graph_sizes,
    block_index,
    block_mask,
    edge_weight,
    step_count,
    branch_weight,
    branch_moment,
    concat_weight,
    concat_moment,
    input_weight,
    input_moment,
    input_second,
    head_weight,
    head_moment,
    head_second,
):
    core = lax.axis_index("branch")
    place = lax.axis_index("dp")
    layers = branch_weight.shape[0]
    labs = labels.shape[0]
    core_arg = core.astype(jnp.int32).reshape(1)
    features_t = features.T
    sides = sides_of(core, place)
    side = sides[0]

    own = cast_weights(branch_weight, concat_weight)
    other = across_cores(own)
    adj, hid = build(block_index, block_mask, graph_sizes, edge_weight, features_t, input_weight)
    out = forward(core_arg, side, graph_sizes, adj, hid, own, other, head_weight, labels, label_mask[None, :], layers)
    kept = layers - 1
    incats, outcats, joins = out[:kept], out[kept : 2 * kept], out[2 * kept : 3 * kept]
    send, keep, ghead, totals, gself, gagg = out[3 * kept :]
    shared = (adj, own, other)

    def back(l, *extra):
        return backward(
            core_arg, side, graph_sizes, shared, (joins[l], incats[l], outcats[l], gself, gagg), extra, layers, l
        )

    for l in reversed(range(1, layers - 1)):
        send, keep, gself, gagg, token = back(l, send, keep, totals)
    upper = Summing(send, keep, sides, totals, [WIDTH] * kept)
    held = lax.optimization_barrier((branch_moment, concat_moment, token))
    other_moments = (across_cores(held[0]), across_cores(held[1]))
    send, keep, token = back(0, features_t, ghead)
    token, _ = step_all(token, [upper], held=other_moments)
    token, (send,) = step_all(token, [upper], ("pass", side, [send], [shaped(*send.shape)]))
    lower = Summing(send, keep, sides, None, [WIDTH, keep.shape[0] - WIDTH])
    while not upper.whole():
        token, _ = step_all(token, [upper, lower])
    totals = upper.totals
    loss_scale = 1.0 / (jnp.maximum(totals[4, 0], 1.0) * labs)
    loss = totals[0, 0] * loss_scale

    moments = (branch_moment, concat_moment, *other_moments)
    weights = (branch_weight, concat_weight)
    scale = loss_scale.reshape(1)
    theirs = (side == core).astype(jnp.int32)

    def offer(group, n):
        return ("choose", theirs, [group.mine[n], group.got[n]], [shaped(WIDTH, WIDTH)])

    kept_out = []
    ortho = []
    for n, l in enumerate(reversed(range(1, layers))):
        token, (swap,) = step_all(token, [lower], offer(upper, n))
        *kept_out, sent, token = muon(
            core_arg, side, scale, upper.mine[n], upper.got[n], across_cores(swap), moments, weights, token, kept_out, ortho, layers, l
        )
        ortho = [across_cores(sent)]
    while not lower.whole():
        token, _ = step_all(token, [lower])
    n_rest = lower.mine[1].shape[0]
    token, (swap, rest) = step_all(
        token, [], offer(lower, 0), ("gather", side, [lower.mine[1], lower.got[1]], [shaped(2 * n_rest, WIDTH)])
    )
    *kept_out, sent, token = muon(
        core_arg, side, scale, lower.mine[0], lower.got[0], across_cores(swap), moments, weights, token, kept_out, ortho, layers, 0
    )
    branch_next, concat_next = kept_out[:2]
    sent = across_cores(sent)
    steps = step_count[0].astype(F32)
    numbers = jnp.stack(
        [loss_scale, 1.0 / (1.0 - jnp.power(first_decay, steps)), 1.0 / (1.0 - jnp.power(second_decay, steps))]
    )
    *ends_out, token = adam(
        core_arg,
        numbers,
        rest,
        across_cores(rest),
        token,
        (input_weight, input_moment, input_second),
        (head_weight, head_moment, head_second),
    )
    branch_new, concat_new, _ = finish(core_arg, weights, *kept_out[2:], token, [sent], [0], layers)
    return (loss, branch_new, branch_next, concat_new, concat_next, *ends_out)


def solution(mesh):
    placed = (
        P("dp", None),
        P(None, "dp"),
        P("dp"),
        P("dp"),
        P("dp", None),
        P("dp", None),
        P("dp", None, None, None),
        P(),
        P(None, "branch", None, None),
        P(None, "branch", None, None),
        P(None, "branch", None),
        P(None, "branch", None),
        P(),
        P(),
        P(),
        P(),
        P(),
        P(),
    )
    return jax.shard_map(
        on_device,
        mesh=mesh,
        in_specs=placed,
        out_specs=(
            P(),
            P(None, "branch", None, None),
            P(None, "branch", None, None),
            P(None, "branch", None),
            P(None, "branch", None),
            P(),
            P(),
            P(),
            P(),
            P(),
            P(),
        ),
        check_vma=False,
    )
```
